128 devices in a mesh: row: 8 (over x, core), col: 16 (over y, z).
Axes of the slice: x: 4, y: 4, z: 4, core: 2. Of those that a mesh axis runs over, the one named last changes fastest.
Arguments:
- phase: float32 [256, 256, 512], P(('row', 'col')), may hold values from -3.140625 to 3.140625
- dirty_map: float32 [256, 512], P(('row', 'col')), may hold values from 0.02 to 2
- pairs: int32 [3072, 2], P(('row', 'col')), may hold values from 0 to 255, as said below
- live: int32 [128], P(('row', 'col')), may hold values from 6 to 24, as said below
Outputs:
- solution: float32 [256, 512], P(('row', 'col'))
The draws below stay inside these ranges and needn't reach their ends.
Inputs may be any that keep to these rules, and one draw needn't show every extreme that they name: Row k of pairs belongs to group g = k // 24 = i * 16 + j. Its first entry p satisfies (p // 2) // 16 == i, its second entry q satisfies (q // 2) % 16 == j, and q != p. Within one group, all first entries with the same p // 2 are equal, and all second entries with the same q // 2 are equal. Rows of a group at or after live[g] are ignored. `live`: some group has all 24 slots listed.
All inputs are finite; a program needn't handle non-finite values.
Results may differ from the reference program's by a relative error of at most 0.0043.
Values may be sent and summed in bfloat16 or wider, within the bound.
A program may use at most 128 MiB of HBM per device.

```python
import math
import jax
import jax.numpy as jnp
from jax import lax

MICS = 256
TILE = 512
TILES_DEV = 2
SLOTS = 24
ITERS = 2
ROW_SIDE = 8
COL_SIDE = 16
TILES = 256


def draw_pairs(key, part):
    key = jax.random.fold_in(key, 11)
    groups = ROW_SIDE * COL_SIDE
    total = groups * SLOTS
    group_id = jnp.arange(total, dtype=jnp.int32) // SLOTS
    row_id = group_id // COL_SIDE
    col_id = group_id % COL_SIDE
    keys = jax.random.split(key, 4)
    col_pick = jax.random.randint(keys[0], (total,), 0, COL_SIDE)
    row_pick = jax.random.randint(keys[1], (total,), 0, ROW_SIDE)
    first_table = jax.random.randint(keys[2], (groups, COL_SIDE), 0, TILES_DEV)
    second_table = jax.random.randint(keys[3], (groups, ROW_SIDE), 0, TILES_DEV)
    first_off = first_table[group_id, col_pick]
    second_off = second_table[group_id, row_pick]
    moved_row = (row_pick + 1) % ROW_SIDE
    moved_off = second_table[group_id, moved_row]
    first_tile = (row_id * COL_SIDE + col_pick) * TILES_DEV + first_off
    second_tile = (row_pick * COL_SIDE + col_id) * TILES_DEV + second_off
    moved_tile = (moved_row * COL_SIDE + col_id) * TILES_DEV + moved_off
    second_tile = jnp.where(second_tile == first_tile, moved_tile, second_tile)
    return jnp.stack([first_tile, second_tile], axis=1).astype(jnp.int32)


def draw_live(key, part):
    key = jax.random.fold_in(key, 23)
    groups = ROW_SIDE * COL_SIDE
    keys = jax.random.split(key, 4)
    counts = jax.random.randint(keys[0], (groups,), SLOTS // 4, SLOTS // 2 + 1)
    heavy_ids = jax.random.randint(keys[1], (4,), 0, groups)
    heavy_counts = jax.random.randint(keys[2], (4,), SLOTS // 2, SLOTS + 1)
    counts = counts.at[heavy_ids].set(heavy_counts)
    busiest = jax.random.randint(keys[3], (), 0, groups)
    counts = counts.at[busiest].set(SLOTS)
    return counts.astype(jnp.int32)


def block_scale(own_key, shape, cuts, low, largest):
    def one(dim, parts):
        draws = jax.random.uniform(jax.random.fold_in(jax.random.fold_in(own_key, 6), dim), (parts,), jnp.float32, low / len(cuts), largest / len(cuts))
        return jnp.repeat(jnp.exp(draws), shape[dim] // parts).reshape((-1,) + (1,) * (len(shape) - dim - 1))

    gain = one(*cuts[0])
    for cut in cuts[1:]:
        gain = gain * one(*cut)
    return gain


def setup_inputs(seed: int = 0) -> dict:
    seeds = jax.random.split(jax.random.key(seed), 5)
    return {
        "phase": jnp.clip(jax.random.uniform(seeds[0], (TILES, MICS, TILE), jnp.float32, -3.140625, 3.140625), -3.140625, 3.140625),
        "dirty_map": jnp.clip(jnp.exp(math.log(2.0) - 4.6051702 * jax.random.uniform(seeds[1], (TILES, TILE), jnp.float32) ** block_scale(seeds[1], (TILES, TILE), ((0, 128),), -0.2, 0.2)), 0.02, 2.0),
        "pairs": draw_pairs(jax.random.fold_in(seeds[4], 71), 0),
        "live": draw_live(jax.random.fold_in(seeds[4], 71), 0),
    }


def steer_pair(phase):
    cosine = jnp.cos(phase).astype(jnp.bfloat16)
    sine_part = jnp.sin(phase).astype(jnp.bfloat16)
    stacked = jnp.concatenate([cosine, sine_part], axis=1)
    turned = jnp.concatenate([sine_part, -cosine], axis=1)
    return stacked, turned


def psf_block(first_steer, second_steer, second_turned):
    gram_real = jnp.dot(first_steer.T, second_steer, preferred_element_type=jnp.float32)
    gram_imag = jnp.dot(first_steer.T, second_turned, preferred_element_type=jnp.float32)
    scale = float(MICS * MICS - MICS)
    return (gram_real * gram_real + gram_imag * gram_imag - float(MICS)) / scale


def reference(phase, dirty_map, pairs, live):
    stacked, turned = steer_pair(phase)
    wide = stacked.astype(jnp.float32)
    power = jnp.sum(wide * wide, axis=1)
    diagonal = (power * power - float(MICS)) / float(MICS * MICS - MICS)
    slots = pairs.shape[0] // live.shape[0]
    highest = lax.Precision.HIGHEST

    def operator(estimate):
        def own_block(tile_index):
            block = psf_block(stacked[tile_index], stacked[tile_index], turned[tile_index])
            return jnp.dot(block, estimate[tile_index], precision=highest)

        product = lax.map(own_block, jnp.arange(TILES).astype(jnp.int32))

        def add_listed(total, slot_index):
            first_tile = pairs[slot_index, 0]
            second_tile = pairs[slot_index, 1]
            listed_flag = (slot_index % slots) < live[slot_index // slots]

            def compute(inner):
                block = psf_block(stacked[first_tile], stacked[second_tile], turned[second_tile])
                inner = inner.at[first_tile].add(jnp.dot(block, estimate[second_tile], precision=highest))
                return inner.at[second_tile].add(jnp.dot(estimate[first_tile], block, precision=highest))

            def unchanged(inner):
                return inner

            return lax.cond(listed_flag, compute, unchanged, total), None

        product, unused = lax.scan(add_listed, product, jnp.arange(pairs.shape[0]).astype(jnp.int32))
        return product

    estimate = jnp.maximum(dirty_map / diagonal, 0.0)
    for sweep in range(ITERS):
        estimate = jnp.maximum(estimate + (dirty_map - operator(estimate)) / diagonal, 0.0)
    return estimate
```

```python
import functools

import jax
import jax.numpy as jnp
from jax import lax
from jax.experimental import pallas as pl
from jax.experimental.pallas import tpu as pltpu
from jax.sharding import PartitionSpec as P

ITERS = 2
MESH = pl.DeviceIdType.MESH
BF = jnp.bfloat16
F32 = jnp.float32
COS = (1.0, -0.49999988079071045, 0.04166648909449577, -0.0013887806562706828,
       2.476993904565461e-05, -2.7079585152023355e-07, 1.7247135941644842e-09)
SIN = (1.0, -0.1666666567325592, 0.008333321660757065, -0.0001984053524211049,
       2.753588887571823e-06, -2.472918936291535e-08, 1.3614490090851916e-10)


def hops(offset):
    return sum(min(step, 4 - step) for step in offset)


OFFSETS = sorted(
    [(a, b, c) for a in range(4) for b in range(4) for c in range(4) if (a, b, c) != (0, 0, 0)],
    key=lambda offset: -hops(offset),
)


def polynomial(square, coefficients):
    total = jnp.full_like(square, coefficients[-1])
    for coefficient in coefficients[-2::-1]:
        total = total * square + coefficient
    return total


def dot(a, b):
    return jnp.dot(a, b, preferred_element_type=F32)


def dot_nt(a, b):
    return lax.dot_general(a, b, (((1,), (1,)), ((), ())), preferred_element_type=F32)


def kernel(
    phase_hbm, dirty_hbm, pairs_hbm, live_hbm, out_ref,
    phase, dirty, pairs, live, cos_b, sin_b, points, esum, ediff,
    send_h, own_h, other_h, send_s, got_s, flat, stack, work,
    rec_send, rec_got, sums_send, sums_got, count_send, count_got, count_f, count_b, eye_perm,
    load_sem, h_send, h_got, x_send, x_got, s_send, s_got, rec_ssem, rec_rsem, sum_ssem, sum_rsem,
    cnt_ssem, cnt_rsem,
):
    tiles, mics, width = phase.shape
    scale = float(mics * mics - mics)
    row, col = lax.axis_index("row"), lax.axis_index("col")
    x, core = lax.div(row, 2), lax.rem(row, 2)
    y, z = lax.div(col, 4), lax.rem(col, 4)
    me = col * 4 + x
    other = row + 1 - 2 * core

    loads = [
        pltpu.make_async_copy(phase_hbm.at[0], phase.at[0], load_sem.at[0]),
        pltpu.make_async_copy(phase_hbm.at[1], phase.at[1], load_sem.at[1]),
        pltpu.make_async_copy(dirty_hbm, dirty, load_sem.at[2]),
        pltpu.make_async_copy(pairs_hbm, pairs, load_sem.at[3]),
        pltpu.make_async_copy(live_hbm, live, load_sem.at[4]),
    ]
    for load in loads:
        load.start()

    barrier = pltpu.get_barrier_semaphore()
    for da, db, dc in OFFSETS:
        pl.semaphore_signal(
            barrier,
            inc=1,
            device_id=(lax.rem(x + da, 4) * 2 + core, lax.rem(y + db, 4) * 4 + lax.rem(z + dc, 4)),
            device_id_type=MESH,
        )
    for da in range(4):
        pl.semaphore_signal(
            barrier, inc=1, device_id=(lax.rem(x + da, 4) * 2 + 1 - core, col), device_id_type=MESH
        )

    lane = lax.broadcasted_iota(jnp.int32, (8, 128), 1)
    sub = lax.broadcasted_iota(jnp.int32, (8, 128), 0)
    chip_lane = col * 4 + x

    def sums_record(estimate):
        record = jnp.zeros((8, 128), F32)
        for t in range(tiles):
            total = jnp.sum(estimate[t : t + 1, :], axis=1, keepdims=True)
            record = jnp.where((sub == 4 + core) & (lane == t * 64 + chip_lane), total, record)
        return record

    def form(it, estimate):
        mats = []
        row_id = lax.broadcasted_iota(jnp.int32, (mics, mics), 0)
        col_id = lax.broadcasted_iota(jnp.int32, (mics, mics), 1)
        for t in range(tiles):
            value = estimate[t : t + 1, :]
            total = jnp.sum(value, axis=1, keepdims=True)
            left = jnp.concatenate(
                [(esum[t] * value).astype(BF), (ediff[t] * -value).astype(BF)], axis=1
            )
            mat = dot(left, points[t])
            mats.append(jnp.where(row_id == col_id, mat - total, mat))
        for half in range(2):
            parts = [m[:, half * 128 : half * 128 + 128].reshape(32, 8, 128) for m in mats]
            send_h[it, pl.ds(half * 32, 32)] = jnp.concatenate(parts, axis=1).astype(BF)

    def send_all(src, dst, ssem, rsem):
        for da, db, dc in OFFSETS:
            px = lax.rem(x + da, 4)
            pc = lax.rem(y + db, 4) * 4 + lax.rem(z + dc, 4)
            pltpu.make_async_remote_copy(
                src_ref=src.at[pc * 4 + px], dst_ref=dst.at[me], send_sem=ssem, recv_sem=rsem,
                device_id=(px * 2 + core, pc), device_id_type=MESH,
            ).start()

    def send_row(src, dst, ssem, rsem):
        for k in range(1, 8):
            pltpu.make_async_remote_copy(
                src_ref=src, dst_ref=dst.at[row], send_sem=ssem, recv_sem=rsem,
                device_id=(lax.rem(row + k, 8), col), device_id_type=MESH,
            ).start()

    def send_col(src, dst, ssem, rsem):
        for k in range(1, 16):
            pltpu.make_async_remote_copy(
                src_ref=src, dst_ref=dst, send_sem=ssem, recv_sem=rsem,
                device_id=(row, lax.rem(col + k, 16)), device_id_type=MESH,
            ).start()

    def wait(ref, sem):
        pltpu.make_async_copy(ref, ref, sem).wait()

    loads[2].wait()
    powers, diags, firsts = [], [], []
    for t in range(tiles):
        loads[t].wait()
        angle = phase[t]
        square = angle * angle
        cosine = polynomial(square, COS).astype(BF)
        sine = (polynomial(square, SIN) * angle).astype(BF)
        cos_b[t] = cosine
        sin_b[t] = sine
        cosine, sine = cosine.astype(F32), sine.astype(F32)
        esum[t] = cosine + sine
        ediff[t] = cosine - sine
        power = jnp.sum(cosine * cosine + sine * sine, axis=0, keepdims=True)
        diag = (power * power - float(mics)) / scale
        powers.append(power)
        diags.append(diag)
        firsts.append(jnp.maximum(dirty[t : t + 1, :] / diag, 0.0))
        points[t] = jnp.concatenate([cosine.T, sine.T], axis=0).astype(BF)
    power = jnp.concatenate(powers, axis=0)
    diag = jnp.concatenate(diags, axis=0)
    estimate = jnp.concatenate(firsts, axis=0)

    loads[3].wait()
    loads[4].wait()
    slots = pairs.shape[1]
    slot_id = lax.broadcasted_iota(jnp.int32, (slots, 128), 0)
    slot_lane = lax.broadcasted_iota(jnp.int32, (slots, 128), 1)
    place = (slot_lane == 32 * lax.rem(row, 4) + slot_id) & (slot_id < live[0])
    numbers = dot((pairs[...] + 1).astype(F32).astype(BF), place.astype(F32).astype(BF))
    half_id = lax.div(row, 4)
    record = sums_record(estimate)
    record = jnp.where(sub == half_id, numbers[0:1, :], record)
    record = jnp.where(sub == 2 + half_id, numbers[1:2, :], record)
    rec_send[0] = record
    rec_got[0, row] = record
    form(0, estimate)
    own_h[0, me] = send_h[0, me]

    raw = lax.broadcasted_iota(jnp.int32, (256, 256), 1)
    raw_row = (raw >> 1) & 7
    placed = (((raw_row + core) & 1) << 7) + ((raw & 1) << 6) + ((raw >> 4) << 2) + (raw_row >> 1)
    eye_perm[...] = (lax.broadcasted_iota(jnp.int32, (256, 256), 0) == placed).astype(F32).astype(BF)

    pl.semaphore_wait(barrier, len(OFFSETS) + 4)

    for it in range(ITERS):
        if it == 0:
            send_row(rec_send.at[0], rec_got.at[0], rec_ssem.at[0], rec_rsem.at[0])
        send_all(send_h.at[it], own_h.at[it], h_send.at[it], h_got.at[it])
        if it:
            send_row(rec_send.at[it], rec_got.at[it], rec_ssem.at[it], rec_rsem.at[it])
        else:
            wait(rec_got.at[0, pl.ds(0, 7)], rec_rsem.at[0])
            record = jnp.sum(rec_got[0], axis=0)
            sums_send[0] = record
            sums_got[0, col] = record
            counts = jnp.zeros((16, 256), F32)
            for half in range(2):
                first = record[half : half + 1, :].astype(jnp.int32) - 1
                second = record[2 + half : 3 + half, :].astype(jnp.int32) - 1
                first_pos = (
                    (((first >> 5) + core) & 1) * 128 + (first & 1) * 64
                    + ((first >> 1) & 15) * 4 + (first >> 6)
                )
                first_pos = jnp.where(first < 0, -1, first_pos)
                second_pos = jnp.where(second < 0, -1, (second >> 5) * 2 + (second & 1))
                first_hot = lax.broadcasted_iota(jnp.int32, (256, 128), 0) == first_pos
                second_hot = lax.broadcasted_iota(jnp.int32, (16, 128), 0) == second_pos
                counts = counts + dot_nt(
                    second_hot.astype(F32).astype(BF), first_hot.astype(F32).astype(BF)
                )
            count_send[...] = counts.astype(BF)
            here = pl.ds(pl.multiple_of(col * 16, 16), 16)
            count_got[here, :] = count_send[...]
            send_col(count_send, count_got.at[here], cnt_ssem, cnt_rsem)
            send_col(sums_send.at[0], sums_got.at[0, col], sum_ssem.at[0], sum_rsem.at[0])

        wait(own_h.at[it, pl.ds(0, 63)], h_got.at[it])
        exchange = pltpu.make_async_remote_copy(
            src_ref=own_h.at[it], dst_ref=other_h.at[it], send_sem=x_send.at[it],
            recv_sem=x_got.at[it], device_id=(other, col), device_id_type=MESH,
        )
        exchange.start()

        def stacked(source, base):
            flat[...] = source.astype(F32).reshape(1024, 128)
            for k in range(16):
                stack[base + (k // 8) * 64 : base + (k // 8) * 64 + 64,
                      (k % 8) * 128 : (k % 8) * 128 + 128] = flat[pl.ds(k, 64, stride=16), :].astype(BF)

        stacked(own_h[it], 0)
        if it == 0:
            wait(count_got.at[pl.ds(0, 240)], cnt_rsem)
            ordered = dot(eye_perm[...], count_got[...])
            here_id = lax.broadcasted_iota(jnp.int32, (128, 256), 0)
            all_id = lax.broadcasted_iota(jnp.int32, (128, 256), 1)
            counts = ordered[0:128, :] + ordered[:, 0:128].T + (here_id == all_id).astype(F32)
            count_f[...] = counts
            count_b[...] = counts.astype(BF)
        work[...] = dot(count_b[:, 0:128], stack[0:128, :])
        exchange.wait_recv()
        stacked(other_h[it], 128)
        total = work[...] + dot(count_b[:, 128:256], stack[128:256, :])
        for k in range(16):
            flat[pl.ds(k, 64, stride=16), :] = total[
                (k // 8) * 64 : (k // 8) * 64 + 64, (k % 8) * 128 : (k % 8) * 128 + 128
            ]
        send_s[it] = flat[...].reshape(64, 16, 128).astype(BF)
        got_s[it, me] = send_s[it, me]
        send_all(send_s.at[it], got_s.at[it], s_send.at[it], s_got.at[it])

        if it:
            wait(rec_got.at[it, pl.ds(0, 7)], rec_rsem.at[it])
            record = jnp.sum(rec_got[it], axis=0)
            sums_send[it] = record
            sums_got[it, col] = record
            send_col(sums_send.at[it], sums_got.at[it, col], sum_ssem.at[it], sum_rsem.at[it])
        wait(sums_got.at[it, pl.ds(0, 15)], sum_rsem.at[it])
        sums = jnp.sum(sums_got[it], axis=0)
        own_sums = jnp.where(core == 0, sums[4:5, :], sums[5:6, :])
        other_sums = jnp.where(core == 0, sums[5:6, :], sums[4:5, :])
        partner = jnp.concatenate([own_sums, other_sums], axis=1)
        spread = [
            jnp.sum(count_f[pl.ds(t * 64 + chip_lane, 1), :] * partner, axis=1, keepdims=True)
            for t in range(tiles)
        ]

        wait(got_s.at[it, pl.ds(0, 63)], s_got.at[it])
        news = []
        for t in range(tiles):
            mat = jnp.concatenate(
                [
                    got_s[it, half * 32 : half * 32 + 32].astype(F32)[:, t * 8 : t * 8 + 8, :].reshape(256, 128)
                    for half in range(2)
                ],
                axis=1,
            ).astype(BF)
            form_sum = jnp.sum(
                esum[t] * dot(mat, cos_b[t]) - ediff[t] * dot(mat, sin_b[t]), axis=0, keepdims=True
            )
            value = (form_sum + spread[t] * (power[t : t + 1] - float(mics))) / scale
            old = estimate[t : t + 1]
            news.append(jnp.maximum(old + (dirty[t : t + 1, :] - value) / diag[t : t + 1], 0.0))
        estimate = jnp.concatenate(news, axis=0)
        if it + 1 < ITERS:
            record = sums_record(estimate)
            rec_send[it + 1] = record
            rec_got[it + 1, row] = record
            form(it + 1, estimate)
            own_h[it + 1, me] = send_h[it + 1, me]

    out_ref[...] = estimate
    for it in range(ITERS):
        wait(send_h.at[it, pl.ds(0, 63)], h_send.at[it])
        wait(other_h.at[it], x_send.at[it])
        wait(send_s.at[it, pl.ds(0, 63)], s_send.at[it])
        wait(rec_got.at[it, pl.ds(0, 7)], rec_ssem.at[it])
        wait(sums_got.at[it, pl.ds(0, 15)], sum_ssem.at[it])
    wait(count_got.at[pl.ds(0, 240)], cnt_ssem)


def on_device(phase, dirty_map, pairs, live):
    tiles, mics, width = phase.shape
    vmem, dma = pltpu.VMEM, pltpu.SemaphoreType.DMA
    blocks = vmem((ITERS, 64, 16, 128), BF)
    return pl.pallas_call(
        kernel,
        out_shape=jax.ShapeDtypeStruct(dirty_map.shape, F32),
        in_specs=[pl.BlockSpec(memory_space=pl.ANY)] * 4,
        out_specs=pl.BlockSpec(memory_space=pltpu.VMEM),
        scratch_shapes=[
            vmem((tiles, mics, width), F32),
            vmem((tiles, width), F32),
            vmem((2, pairs.shape[0]), jnp.int32),
            pltpu.SMEM((1,), jnp.int32),
            vmem((tiles, mics, width), BF),
            vmem((tiles, mics, width), BF),
            vmem((tiles, 2 * width, mics), BF),
            vmem((tiles, mics, width), F32),
            vmem((tiles, mics, width), F32),
            blocks, blocks, blocks, blocks, blocks,
            vmem((1024, 128), F32),
            vmem((256, 1024), BF),
            vmem((128, 1024), F32),
            vmem((ITERS, 8, 128), F32),
            vmem((ITERS, 8, 8, 128), F32),
            vmem((ITERS, 8, 128), F32),
            vmem((ITERS, 16, 8, 128), F32),
            vmem((16, 256), BF),
            vmem((256, 256), BF),
            vmem((128, 256), F32),
            vmem((128, 256), BF),
            vmem((256, 256), BF),
            dma((5,)),
            dma((ITERS,)), dma((ITERS,)), dma((ITERS,)), dma((ITERS,)), dma((ITERS,)), dma((ITERS,)),
            dma((ITERS,)), dma((ITERS,)), dma((ITERS,)), dma((ITERS,)),
            dma, dma,
        ],
        compiler_params=pltpu.CompilerParams(
            collective_id=0, has_side_effects=True, vmem_limit_bytes=48 << 20
        ),
    )(phase, dirty_map, pairs.T, live)


def solution(mesh):
    in_specs = (
        P(("row", "col"), None, None),
        P(("row", "col"), None),
        P(("row", "col"), None),
        P(("row", "col")),
    )
    out_specs = P(("row", "col"), None)
    return jax.shard_map(
        on_device, mesh=mesh, in_specs=in_specs, out_specs=out_specs, check_vma=False
    )
```

```python
import functools

import jax
import jax.numpy as jnp
from jax import lax
from jax.experimental import pallas as pl
from jax.experimental.pallas import tpu as pltpu
from jax.sharding import PartitionSpec as P

ITERS = 2
MESH = pl.DeviceIdType.MESH
BF = jnp.bfloat16
F32 = jnp.float32
COS = (1.0, -0.49999988079071045, 0.04166648909449577, -0.0013887806562706828,
       2.476993904565461e-05, -2.7079585152023355e-07, 1.7247135941644842e-09)
SIN = (1.0, -0.1666666567325592, 0.008333321660757065, -0.0001984053524211049,
       2.753588887571823e-06, -2.472918936291535e-08, 1.3614490090851916e-10)


def hops(offset):
    return sum(min(step, 4 - step) for step in offset)


OFFSETS = sorted(
    [(a, b, c) for a in range(4) for b in range(4) for c in range(4) if (a, b, c) != (0, 0, 0)],
    key=lambda offset: -hops(offset),
)


def polynomial(square, coefficients):
    total = jnp.full_like(square, coefficients[-1])
    for coefficient in coefficients[-2::-1]:
        total = total * square + coefficient
    return total


def dot(a, b):
    return jnp.dot(a, b, preferred_element_type=F32)


def dot_nt(a, b):
    return lax.dot_general(a, b, (((1,), (1,)), ((), ())), preferred_element_type=F32)


def kernel(
    phase_hbm, dirty_hbm, pairs_hbm, live_hbm, out_ref,
    phase, dirty, pairs, live, cos_b, sin_b, points, esum, ediff,
    send_h, own_h, other_h, send_s, got_s, flat, stack, work,
    rec_send, rec_got, sums_send, sums_got, part_send, part_got, count_send, count_got, count_f, count_b,
    eye_perm,
    load_sem, h_send, h_got, x_send, x_got, s_send, s_got, rec_ssem, rec_rsem, sum_ssem, sum_rsem,
    part_ssem, part_rsem, cnt_ssem, cnt_rsem,
):
    tiles, mics, width = phase.shape
    scale = float(mics * mics - mics)
    row, col = lax.axis_index("row"), lax.axis_index("col")
    x, core = lax.div(row, 2), lax.rem(row, 2)
    y, z = lax.div(col, 4), lax.rem(col, 4)
    me = col * 4 + x
    other = row + 1 - 2 * core

    loads = [
        pltpu.make_async_copy(phase_hbm.at[0], phase.at[0], load_sem.at[0]),
        pltpu.make_async_copy(phase_hbm.at[1], phase.at[1], load_sem.at[1]),
        pltpu.make_async_copy(dirty_hbm, dirty, load_sem.at[2]),
        pltpu.make_async_copy(pairs_hbm, pairs, load_sem.at[3]),
        pltpu.make_async_copy(live_hbm, live, load_sem.at[4]),
    ]
    for load in loads:
        load.start()

    barrier = pltpu.get_barrier_semaphore()
    for da, db, dc in OFFSETS:
        pl.semaphore_signal(
            barrier,
            inc=1,
            device_id=(lax.rem(x + da, 4) * 2 + core, lax.rem(y + db, 4) * 4 + lax.rem(z + dc, 4)),
            device_id_type=MESH,
        )
    for da in range(4):
        pl.semaphore_signal(
            barrier, inc=1, device_id=(lax.rem(x + da, 4) * 2 + 1 - core, col), device_id_type=MESH
        )

    lane = lax.broadcasted_iota(jnp.int32, (8, 128), 1)
    sub = lax.broadcasted_iota(jnp.int32, (8, 128), 0)
    chip_lane = col * 4 + x

    def sums_record(estimate):
        record = jnp.zeros((8, 128), F32)
        for t in range(tiles):
            total = jnp.sum(estimate[t : t + 1, :], axis=1, keepdims=True)
            record = jnp.where((sub == 4 + core) & (lane == t * 64 + chip_lane), total, record)
        return record

    def form(it, estimate):
        mats = []
        row_id = lax.broadcasted_iota(jnp.int32, (mics, mics), 0)
        col_id = lax.broadcasted_iota(jnp.int32, (mics, mics), 1)
        for t in range(tiles):
            value = estimate[t : t + 1, :]
            total = jnp.sum(value, axis=1, keepdims=True)
            left = jnp.concatenate(
                [(esum[t] * value).astype(BF), (ediff[t] * -value).astype(BF)], axis=1
            )
            mat = dot(left, points[t])
            mats.append(jnp.where(row_id == col_id, mat - total, mat))
        for half in range(2):
            parts = [m[:, half * 128 : half * 128 + 128].reshape(32, 8, 128) for m in mats]
            send_h[it, pl.ds(half * 32, 32)] = jnp.concatenate(parts, axis=1).astype(BF)

    def send_all(src, dst, ssem, rsem):
        for da, db, dc in OFFSETS:
            px = lax.rem(x + da, 4)
            pc = lax.rem(y + db, 4) * 4 + lax.rem(z + dc, 4)
            pltpu.make_async_remote_copy(
                src_ref=src.at[pc * 4 + px], dst_ref=dst.at[me], send_sem=ssem, recv_sem=rsem,
                device_id=(px * 2 + core, pc), device_id_type=MESH,
            ).start()

    def send_row(src, dst, ssem, rsem):
        for k in (4, 5, 3, 2, 6, 7, 1):
            pltpu.make_async_remote_copy(
                src_ref=src, dst_ref=dst.at[row], send_sem=ssem, recv_sem=rsem,
                device_id=(lax.rem(row + k, 8), col), device_id_type=MESH,
            ).start()

    def send_col(src, dst, ssem, rsem):
        for da, db, dc in OFFSETS:
            if da == 0:
                pltpu.make_async_remote_copy(
                    src_ref=src, dst_ref=dst, send_sem=ssem, recv_sem=rsem,
                    device_id=(row, lax.rem(y + db, 4) * 4 + lax.rem(z + dc, 4)), device_id_type=MESH,
                ).start()

    def wait(ref, sem):
        pltpu.make_async_copy(ref, ref, sem).wait()

    loads[2].wait()
    powers, diags, firsts = [], [], []
    for t in range(tiles):
        loads[t].wait()
        angle = phase[t]
        square = angle * angle
        cosine = polynomial(square, COS).astype(BF)
        sine = (polynomial(square, SIN) * angle).astype(BF)
        cos_b[t] = cosine
        sin_b[t] = sine
        cosine, sine = cosine.astype(F32), sine.astype(F32)
        esum[t] = cosine + sine
        ediff[t] = cosine - sine
        power = jnp.sum(cosine * cosine + sine * sine, axis=0, keepdims=True)
        diag = (power * power - float(mics)) / scale
        powers.append(power)
        diags.append(diag)
        firsts.append(jnp.maximum(dirty[t : t + 1, :] / diag, 0.0))
        points[t] = jnp.concatenate([cosine.T, sine.T], axis=0).astype(BF)
    power = jnp.concatenate(powers, axis=0)
    diag = jnp.concatenate(diags, axis=0)
    estimate = jnp.concatenate(firsts, axis=0)

    loads[3].wait()
    loads[4].wait()
    slots = pairs.shape[1]
    first, second = pairs[0:1, :], pairs[1:2, :]
    first_lane = (first & 1) * 64 + ((first >> 1) & 15) * 4 + (first >> 6)
    second_row = (second >> 5) * 2 + (second & 1)
    listed = lax.broadcasted_iota(jnp.int32, (128, slots), 1) < live[0]
    first_hot = (lax.broadcasted_iota(jnp.int32, (128, slots), 0) == first_lane) & listed
    second_hot = lax.broadcasted_iota(jnp.int32, (16, slots), 0) == second_row
    part_send[...] = dot_nt(
        second_hot.astype(F32).astype(BF), first_hot.astype(F32).astype(BF)
    ).astype(BF)
    part_got[row] = part_send[...]
    record = sums_record(estimate)
    rec_send[0] = record
    rec_got[0, row] = record
    form(0, estimate)

    raw = lax.broadcasted_iota(jnp.int32, (256, 256), 1)
    raw_row = (raw >> 1) & 7
    placed = (((raw_row + core) & 1) << 7) + ((raw & 1) << 6) + ((raw >> 4) << 2) + (raw_row >> 1)
    eye_perm[...] = (lax.broadcasted_iota(jnp.int32, (256, 256), 0) == placed).astype(F32).astype(BF)

    pl.semaphore_wait(barrier, len(OFFSETS) + 4)

    for it in range(ITERS):
        if it == 0:
            send_row(part_send, part_got, part_ssem, part_rsem)
        send_all(send_h.at[it], own_h.at[it], h_send.at[it], h_got.at[it])
        send_row(rec_send.at[it], rec_got.at[it], rec_ssem.at[it], rec_rsem.at[it])
        own_h[it, me] = send_h[it, me]
        if it == 0:
            wait(part_got.at[pl.ds(0, 7)], part_rsem)
            by_core = [
                sum(part_got[2 * k + c].astype(F32) for k in range(4)).astype(BF) for c in range(2)
            ]
            count_send[:, 0:128] = jnp.where(core == 0, by_core[0], by_core[1])
            count_send[:, 128:256] = jnp.where(core == 0, by_core[1], by_core[0])
            here = pl.ds(pl.multiple_of(col * 16, 16), 16)
            count_got[here, :] = count_send[...]
            send_col(count_send, count_got.at[here], cnt_ssem, cnt_rsem)

        wait(own_h.at[it, pl.ds(0, 63)], h_got.at[it])
        exchange = pltpu.make_async_remote_copy(
            src_ref=own_h.at[it], dst_ref=other_h.at[it], send_sem=x_send.at[it],
            recv_sem=x_got.at[it], device_id=(other, col), device_id_type=MESH,
        )
        exchange.start()
        wait(rec_got.at[it, pl.ds(0, 7)], rec_rsem.at[it])
        record = jnp.sum(rec_got[it], axis=0)
        sums_send[it] = record
        sums_got[it, col] = record
        send_col(sums_send.at[it], sums_got.at[it, col], sum_ssem.at[it], sum_rsem.at[it])

        def stacked(source, base):
            turned = jnp.swapaxes(source, 0, 1)
            for k in range(16):
                stack[base + (k // 8) * 64 : base + (k // 8) * 64 + 64,
                      (k % 8) * 128 : (k % 8) * 128 + 128] = turned[k]

        stacked(own_h[it], 0)
        if it == 0:
            wait(count_got.at[pl.ds(0, 240)], cnt_rsem)
            ordered = dot(eye_perm[...], count_got[...])
            here_id = lax.broadcasted_iota(jnp.int32, (128, 256), 0)
            all_id = lax.broadcasted_iota(jnp.int32, (128, 256), 1)
            counts = ordered[0:128, :] + ordered[:, 0:128].T + (here_id == all_id).astype(F32)
            count_f[...] = counts
            count_b[...] = counts.astype(BF)
        work[...] = dot(count_b[:, 0:128], stack[0:128, :])
        exchange.wait_recv()
        stacked(other_h[it], 128)
        total = work[...] + dot(count_b[:, 128:256], stack[128:256, :])
        cut = [
            total[(k // 8) * 64 : (k // 8) * 64 + 64, (k % 8) * 128 : (k % 8) * 128 + 128]
            for k in range(16)
        ]
        send_s[it] = jnp.swapaxes(jnp.stack(cut, axis=0), 0, 1).astype(BF)
        send_all(send_s.at[it], got_s.at[it], s_send.at[it], s_got.at[it])
        got_s[it, me] = send_s[it, me]
        wait(sums_got.at[it, pl.ds(0, 15)], sum_rsem.at[it])
        sums = jnp.sum(sums_got[it], axis=0)
        own_sums = jnp.where(core == 0, sums[4:5, :], sums[5:6, :])
        other_sums = jnp.where(core == 0, sums[5:6, :], sums[4:5, :])
        partner = jnp.concatenate([own_sums, other_sums], axis=1)
        spread = [
            jnp.sum(count_f[pl.ds(t * 64 + chip_lane, 1), :] * partner, axis=1, keepdims=True)
            for t in range(tiles)
        ]

        wait(got_s.at[it, pl.ds(0, 63)], s_got.at[it])
        news = []
        for t in range(tiles):
            mat = jnp.concatenate(
                [
                    got_s[it, half * 32 : half * 32 + 32].astype(F32)[:, t * 8 : t * 8 + 8, :].reshape(256, 128)
                    for half in range(2)
                ],
                axis=1,
            ).astype(BF)
            form_sum = jnp.sum(
                esum[t] * dot(mat, cos_b[t]) - ediff[t] * dot(mat, sin_b[t]), axis=0, keepdims=True
            )
            value = (form_sum + spread[t] * (power[t : t + 1] - float(mics))) / scale
            old = estimate[t : t + 1]
            news.append(jnp.maximum(old + (dirty[t : t + 1, :] - value) / diag[t : t + 1], 0.0))
        estimate = jnp.concatenate(news, axis=0)
        if it + 1 < ITERS:
            record = sums_record(estimate)
            rec_send[it + 1] = record
            rec_got[it + 1, row] = record
            form(it + 1, estimate)

    out_ref[...] = estimate
    for it in range(ITERS):
        wait(send_h.at[it, pl.ds(0, 63)], h_send.at[it])
        wait(other_h.at[it], x_send.at[it])
        wait(send_s.at[it, pl.ds(0, 63)], s_send.at[it])
        wait(rec_got.at[it, pl.ds(0, 7)], rec_ssem.at[it])
        wait(sums_got.at[it, pl.ds(0, 15)], sum_ssem.at[it])
    wait(count_got.at[pl.ds(0, 240)], cnt_ssem)
    wait(part_got.at[pl.ds(0, 7)], part_ssem)


def on_device(phase, dirty_map, pairs, live):
    tiles, mics, width = phase.shape
    vmem, dma = pltpu.VMEM, pltpu.SemaphoreType.DMA
    blocks = vmem((ITERS, 64, 16, 128), BF)
    return pl.pallas_call(
        kernel,
        out_shape=jax.ShapeDtypeStruct(dirty_map.shape, F32),
        in_specs=[pl.BlockSpec(memory_space=pl.ANY)] * 4,
        out_specs=pl.BlockSpec(memory_space=pltpu.VMEM),
        scratch_shapes=[
            vmem((tiles, mics, width), F32),
            vmem((tiles, width), F32),
            vmem((2, pairs.shape[0]), jnp.int32),
            pltpu.SMEM((1,), jnp.int32),
            vmem((tiles, mics, width), BF),
            vmem((tiles, mics, width), BF),
            vmem((tiles, 2 * width, mics), BF),
            vmem((tiles, mics, width), F32),
            vmem((tiles, mics, width), F32),
            blocks, blocks, blocks, blocks, blocks,
            vmem((1024, 128), F32),
            vmem((256, 1024), BF),
            vmem((128, 1024), F32),
            vmem((ITERS, 8, 128), F32),
            vmem((ITERS, 8, 8, 128), F32),
            vmem((ITERS, 8, 128), F32),
            vmem((ITERS, 16, 8, 128), F32),
            vmem((16, 128), BF),
            vmem((8, 16, 128), BF),
            vmem((16, 256), BF),
            vmem((256, 256), BF),
            vmem((128, 256), F32),
            vmem((128, 256), BF),
            vmem((256, 256), BF),
            dma((5,)),
            dma((ITERS,)), dma((ITERS,)), dma((ITERS,)), dma((ITERS,)), dma((ITERS,)), dma((ITERS,)),
            dma((ITERS,)), dma((ITERS,)), dma((ITERS,)), dma((ITERS,)),
            dma, dma, dma, dma,
        ],
        compiler_params=pltpu.CompilerParams(
            collective_id=0, has_side_effects=True, vmem_limit_bytes=48 << 20
        ),
    )(*[pltpu.with_memory_space_constraint(v, pltpu.HBM) for v in (phase, dirty_map, pairs.T)], live)


def solution(mesh):
    in_specs = (
        P(("row", "col"), None, None),
        P(("row", "col"), None),
        P(("row", "col"), None),
        P(("row", "col")),
    )
    out_specs = P(("row", "col"), None)
    return jax.shard_map(
        on_device, mesh=mesh, in_specs=in_specs, out_specs=out_specs, check_vma=False
    )
```

```python
import functools

import jax
import jax.numpy as jnp
from jax import lax
from jax.experimental import pallas as pl
from jax.experimental.pallas import tpu as pltpu
from jax.sharding import PartitionSpec as P

ITERS = 2
MESH = pl.DeviceIdType.MESH
BF = jnp.bfloat16
F32 = jnp.float32
HALF_COS = (0.9999999403953552, -0.1249997615814209, 0.002603973960503936, -2.1646421373588964e-05,
            9.044592985674171e-08)
HALF_SIN = (0.5, -0.020833322778344154, 0.0002604078617878258, -1.5475848158530425e-06,
            5.0883919300304115e-09)


def hops(offset):
    return sum(min(step, 4 - step) for step in offset)


OFFSETS = sorted(
    [(a, b, c) for a in range(4) for b in range(4) for c in range(4) if (a, b, c) != (0, 0, 0)],
    key=lambda offset: -hops(offset),
)


def polynomial(square, coefficients):
    total = jnp.full_like(square, coefficients[-1])
    for coefficient in coefficients[-2::-1]:
        total = total * square + coefficient
    return total


def dot(a, b):
    return jnp.dot(a, b, preferred_element_type=F32)


def dot_nt(a, b):
    return lax.dot_general(a, b, (((1,), (1,)), ((), ())), preferred_element_type=F32)


def kernel(
    phase_hbm, dirty_hbm, pairs_hbm, live_hbm, out_ref,
    phase, dirty, pairs, live, cos_b, sin_b, points, esum, ediff,
    send_h, own_h, other_h, send_s, got_s, flat, stack, work,
    rec_send, rec_got, sums_send, sums_got, part_send, part_got, count_send, count_got, count_f, count_b,
    eye_perm,
    load_sem, h_send, h_got, x_send, x_got, s_send, s_got, rec_ssem, rec_rsem, sum_ssem, sum_rsem,
    part_ssem, part_rsem, cnt_ssem, cnt_rsem,
):
    tiles, mics, width = phase.shape
    scale = float(mics * mics - mics)
    row, col = lax.axis_index("row"), lax.axis_index("col")
    x, core = lax.div(row, 2), lax.rem(row, 2)
    y, z = lax.div(col, 4), lax.rem(col, 4)
    me = col * 4 + x
    other = row + 1 - 2 * core

    barrier = pltpu.get_barrier_semaphore()

    def greet(px, pc, pcore):
        pl.semaphore_signal(
            barrier, inc=1, device_id=(px * 2 + pcore, pc), device_id_type=MESH
        )

    for offset in OFFSETS[:22]:
        px, pc = lax.rem(x + offset[0], 4), lax.rem(y + offset[1], 4) * 4 + lax.rem(z + offset[2], 4)
        greet(px, pc, core)

    loads = [
        pltpu.make_async_copy(phase_hbm.at[0], phase.at[0], load_sem.at[0]),
        pltpu.make_async_copy(phase_hbm.at[1], phase.at[1], load_sem.at[1]),
        pltpu.make_async_copy(dirty_hbm, dirty, load_sem.at[2]),
        pltpu.make_async_copy(pairs_hbm, pairs, load_sem.at[3]),
        pltpu.make_async_copy(live_hbm, live, load_sem.at[4]),
    ]
    for load in loads:
        load.start()

    for offset in OFFSETS[22:]:
        px, pc = lax.rem(x + offset[0], 4), lax.rem(y + offset[1], 4) * 4 + lax.rem(z + offset[2], 4)
        greet(px, pc, core)
    for da in range(4):
        greet(lax.rem(x + da, 4), col, 1 - core)

    lane = lax.broadcasted_iota(jnp.int32, (8, 128), 1)
    sub = lax.broadcasted_iota(jnp.int32, (8, 128), 0)
    chip_lane = col * 4 + x

    def sums_record(estimate):
        record = jnp.zeros((8, 128), F32)
        for t in range(tiles):
            total = jnp.sum(estimate[t : t + 1, :], axis=1, keepdims=True)
            record = jnp.where((sub == 4 + core) & (lane == t * 64 + chip_lane), total, record)
        return record

    def form(it, estimate):
        mats = []
        row_id = lax.broadcasted_iota(jnp.int32, (mics, mics), 0)
        col_id = lax.broadcasted_iota(jnp.int32, (mics, mics), 1)
        for t in range(tiles):
            value = estimate[t : t + 1, :]
            total = jnp.sum(value, axis=1, keepdims=True)
            left = jnp.concatenate(
                [(esum[t] * value).astype(BF), (ediff[t] * -value).astype(BF)], axis=1
            )
            mat = dot(left, points[t])
            mats.append(jnp.where(row_id == col_id, mat - total, mat))
        for half in range(2):
            parts = [m[:, half * 128 : half * 128 + 128].reshape(32, 8, 128) for m in mats]
            send_h[it, pl.ds(half * 32, 32)] = jnp.concatenate(parts, axis=1).astype(BF)

    def send_all(src, dst, ssem, rsem):
        for da, db, dc in OFFSETS:
            px = lax.rem(x + da, 4)
            pc = lax.rem(y + db, 4) * 4 + lax.rem(z + dc, 4)
            pltpu.make_async_remote_copy(
                src_ref=src.at[pc * 4 + px], dst_ref=dst.at[me], send_sem=ssem, recv_sem=rsem,
                device_id=(px * 2 + core, pc), device_id_type=MESH,
            ).start()

    def send_row(src, dst, ssem, rsem):
        for k in (4, 5, 3, 2, 6, 7, 1):
            pltpu.make_async_remote_copy(
                src_ref=src, dst_ref=dst.at[row], send_sem=ssem, recv_sem=rsem,
                device_id=(lax.rem(row + k, 8), col), device_id_type=MESH,
            ).start()

    def send_col(src, dst, ssem, rsem):
        for da, db, dc in OFFSETS:
            if da == 0:
                pltpu.make_async_remote_copy(
                    src_ref=src, dst_ref=dst, send_sem=ssem, recv_sem=rsem,
                    device_id=(row, lax.rem(y + db, 4) * 4 + lax.rem(z + dc, 4)), device_id_type=MESH,
                ).start()

    def wait(ref, sem):
        pltpu.make_async_copy(ref, ref, sem).wait()

    loads[2].wait()
    powers, diags, firsts = [], [], []
    for t in range(tiles):
        loads[t].wait()
        angle = phase[t]
        square = angle * angle
        half_sine = polynomial(square, HALF_SIN) * angle
        twice = half_sine + half_sine
        cosine = (1.0 - twice * half_sine).astype(BF)
        sine = (twice * polynomial(square, HALF_COS)).astype(BF)
        cos_b[t] = cosine
        sin_b[t] = sine
        cosine, sine = cosine.astype(F32), sine.astype(F32)
        esum[t] = cosine + sine
        ediff[t] = cosine - sine
        power = jnp.sum(cosine * cosine + sine * sine, axis=0, keepdims=True)
        diag = (power * power - float(mics)) / scale
        powers.append(power)
        diags.append(diag)
        firsts.append(jnp.maximum(dirty[t : t + 1, :] / diag, 0.0))
        points[t] = jnp.concatenate([cosine.T, sine.T], axis=0).astype(BF)
    power = jnp.concatenate(powers, axis=0)
    diag = jnp.concatenate(diags, axis=0)
    estimate = jnp.concatenate(firsts, axis=0)

    loads[3].wait()
    loads[4].wait()
    slots = pairs.shape[1]
    first, second = pairs[0:1, :], pairs[1:2, :]
    first_lane = (first & 1) * 64 + ((first >> 1) & 15) * 4 + (first >> 6)
    second_row = (second >> 5) * 2 + (second & 1)
    listed = lax.broadcasted_iota(jnp.int32, (128, slots), 1) < live[0]
    first_hot = (lax.broadcasted_iota(jnp.int32, (128, slots), 0) == first_lane) & listed
    second_hot = lax.broadcasted_iota(jnp.int32, (16, slots), 0) == second_row
    part_send[...] = dot_nt(
        second_hot.astype(F32).astype(BF), first_hot.astype(F32).astype(BF)
    ).astype(BF)
    part_got[row] = part_send[...]
    record = sums_record(estimate)
    rec_send[0] = record
    rec_got[0, row] = record
    form(0, estimate)

    raw = lax.broadcasted_iota(jnp.int32, (256, 256), 1)
    raw_row = (raw >> 1) & 7
    placed = (((raw_row + core) & 1) << 7) + ((raw & 1) << 6) + ((raw >> 4) << 2) + (raw_row >> 1)
    eye_perm[...] = (lax.broadcasted_iota(jnp.int32, (256, 256), 0) == placed).astype(F32).astype(BF)

    pl.semaphore_wait(barrier, len(OFFSETS) + 4)

    for it in range(ITERS):
        if it == 0:
            send_row(part_send, part_got, part_ssem, part_rsem)
        send_all(send_h.at[it], own_h.at[it], h_send.at[it], h_got.at[it])
        if it:
            send_row(rec_send.at[it], rec_got.at[it], rec_ssem.at[it], rec_rsem.at[it])
        own_h[it, me] = send_h[it, me]
        if it == 0:
            wait(part_got.at[pl.ds(0, 7)], part_rsem)
            by_core = [
                sum(part_got[2 * k + c].astype(F32) for k in range(4)).astype(BF) for c in range(2)
            ]
            count_send[:, 0:128] = jnp.where(core == 0, by_core[0], by_core[1])
            count_send[:, 128:256] = jnp.where(core == 0, by_core[1], by_core[0])
            here = pl.ds(pl.multiple_of(col * 16, 16), 16)
            count_got[here, :] = count_send[...]
            send_col(count_send, count_got.at[here], cnt_ssem, cnt_rsem)
            send_row(rec_send.at[it], rec_got.at[it], rec_ssem.at[it], rec_rsem.at[it])

        wait(own_h.at[it, pl.ds(0, 63)], h_got.at[it])
        exchange = pltpu.make_async_remote_copy(
            src_ref=own_h.at[it], dst_ref=other_h.at[it], send_sem=x_send.at[it],
            recv_sem=x_got.at[it], device_id=(other, col), device_id_type=MESH,
        )
        exchange.start()
        wait(rec_got.at[it, pl.ds(0, 7)], rec_rsem.at[it])
        record = jnp.sum(rec_got[it], axis=0)
        sums_send[it] = record
        sums_got[it, col] = record
        send_col(sums_send.at[it], sums_got.at[it, col], sum_ssem.at[it], sum_rsem.at[it])

        def stacked(source, base):
            turned = jnp.swapaxes(source, 0, 1)
            for k in range(16):
                stack[base + (k // 8) * 64 : base + (k // 8) * 64 + 64,
                      (k % 8) * 128 : (k % 8) * 128 + 128] = turned[k]

        stacked(own_h[it], 0)
        if it:
            work[...] = dot(count_b[:, 0:128], stack[0:128, :])
        exchange.wait_recv()
        stacked(other_h[it], 128)
        if it:
            total = work[...] + dot(count_b[:, 128:256], stack[128:256, :])
        else:
            wait(count_got.at[pl.ds(0, 240)], cnt_rsem)
            ordered = dot(eye_perm[...], count_got[...])
            here_id = lax.broadcasted_iota(jnp.int32, (128, 256), 0)
            all_id = lax.broadcasted_iota(jnp.int32, (128, 256), 1)
            counts = ordered[0:128, :] + ordered[:, 0:128].T + (here_id == all_id).astype(F32)
            count_f[...] = counts
            count_b[...] = counts.astype(BF)
            total = dot(count_b[...], stack[...])
        cut = [
            total[(k // 8) * 64 : (k // 8) * 64 + 64, (k % 8) * 128 : (k % 8) * 128 + 128]
            for k in range(16)
        ]
        send_s[it] = jnp.swapaxes(jnp.stack(cut, axis=0), 0, 1).astype(BF)
        send_all(send_s.at[it], got_s.at[it], s_send.at[it], s_got.at[it])
        got_s[it, me] = send_s[it, me]
        wait(sums_got.at[it, pl.ds(0, 15)], sum_rsem.at[it])
        sums = jnp.sum(sums_got[it], axis=0)
        own_sums = jnp.where(core == 0, sums[4:5, :], sums[5:6, :])
        other_sums = jnp.where(core == 0, sums[5:6, :], sums[4:5, :])
        partner = jnp.concatenate([own_sums, other_sums], axis=1)
        spread = [
            jnp.sum(count_f[pl.ds(t * 64 + chip_lane, 1), :] * partner, axis=1, keepdims=True)
            for t in range(tiles)
        ]

        wait(got_s.at[it, pl.ds(0, 63)], s_got.at[it])
        news = []
        for t in range(tiles):
            mat = jnp.concatenate(
                [
                    got_s[it, half * 32 : half * 32 + 32].astype(F32)[:, t * 8 : t * 8 + 8, :].reshape(256, 128)
                    for half in range(2)
                ],
                axis=1,
            ).astype(BF)
            form_sum = jnp.sum(
                esum[t] * dot(mat, cos_b[t]) - ediff[t] * dot(mat, sin_b[t]), axis=0, keepdims=True
            )
            value = (form_sum + spread[t] * (power[t : t + 1] - float(mics))) / scale
            old = estimate[t : t + 1]
            news.append(jnp.maximum(old + (dirty[t : t + 1, :] - value) / diag[t : t + 1], 0.0))
        estimate = jnp.concatenate(news, axis=0)
        if it + 1 < ITERS:
            record = sums_record(estimate)
            rec_send[it + 1] = record
            rec_got[it + 1, row] = record
            form(it + 1, estimate)

    out_ref[...] = estimate
    for it in range(ITERS):
        wait(send_h.at[it, pl.ds(0, 63)], h_send.at[it])
        wait(other_h.at[it], x_send.at[it])
        wait(send_s.at[it, pl.ds(0, 63)], s_send.at[it])
        wait(rec_got.at[it, pl.ds(0, 7)], rec_ssem.at[it])
        wait(sums_got.at[it, pl.ds(0, 15)], sum_ssem.at[it])
    wait(count_got.at[pl.ds(0, 240)], cnt_ssem)
    wait(part_got.at[pl.ds(0, 7)], part_ssem)


def on_device(phase, dirty_map, pairs, live):
    tiles, mics, width = phase.shape
    vmem, dma = pltpu.VMEM, pltpu.SemaphoreType.DMA
    blocks = vmem((ITERS, 64, 16, 128), BF)
    return pl.pallas_call(
        kernel,
        out_shape=jax.ShapeDtypeStruct(dirty_map.shape, F32),
        in_specs=[pl.BlockSpec(memory_space=pl.ANY)] * 4,
        out_specs=pl.BlockSpec(memory_space=pltpu.VMEM),
        scratch_shapes=[
            vmem((tiles, mics, width), F32),
            vmem((tiles, width), F32),
            vmem((2, pairs.shape[0]), jnp.int32),
            pltpu.SMEM((1,), jnp.int32),
            vmem((tiles, mics, width), BF),
            vmem((tiles, mics, width), BF),
            vmem((tiles, 2 * width, mics), BF),
            vmem((tiles, mics, width), F32),
            vmem((tiles, mics, width), F32),
            blocks, blocks, blocks, blocks, blocks,
            vmem((1024, 128), F32),
            vmem((256, 1024), BF),
            vmem((128, 1024), F32),
            vmem((ITERS, 8, 128), F32),
            vmem((ITERS, 8, 8, 128), F32),
            vmem((ITERS, 8, 128), F32),
            vmem((ITERS, 16, 8, 128), F32),
            vmem((16, 128), BF),
            vmem((8, 16, 128), BF),
            vmem((16, 256), BF),
            vmem((256, 256), BF),
            vmem((128, 256), F32),
            vmem((128, 256), BF),
            vmem((256, 256), BF),
            dma((5,)),
            dma((ITERS,)), dma((ITERS,)), dma((ITERS,)), dma((ITERS,)), dma((ITERS,)), dma((ITERS,)),
            dma((ITERS,)), dma((ITERS,)), dma((ITERS,)), dma((ITERS,)),
            dma, dma, dma, dma,
        ],
        compiler_params=pltpu.CompilerParams(
            collective_id=0, has_side_effects=True, vmem_limit_bytes=48 << 20
        ),
    )(*[pltpu.with_memory_space_constraint(v, pltpu.HBM) for v in (phase, dirty_map, pairs.T)], live)


def solution(mesh):
    in_specs = (
        P(("row", "col"), None, None),
        P(("row", "col"), None),
        P(("row", "col"), None),
        P(("row", "col")),
    )
    out_specs = P(("row", "col"), None)
    return jax.shard_map(
        on_device, mesh=mesh, in_specs=in_specs, out_specs=out_specs, check_vma=False
    )
```

```python
import functools

import jax
import jax.numpy as jnp
from jax import lax
from jax.experimental import pallas as pl
from jax.experimental.pallas import tpu as pltpu
from jax.sharding import PartitionSpec as P

ITERS = 2
MESH = pl.DeviceIdType.MESH
BF = jnp.bfloat16
F32 = jnp.float32
HALF_COS = (0.9999999403953552, -0.1249997615814209, 0.002603973960503936, -2.1646421373588964e-05,
            9.044592985674171e-08)
HALF_SIN = (0.5, -0.020833322778344154, 0.0002604078617878258, -1.5475848158530425e-06,
            5.0883919300304115e-09)


def hops(offset):
    return sum(min(step, 4 - step) for step in offset)


OFFSETS = sorted(
    [(a, b, c) for a in range(4) for b in range(4) for c in range(4) if (a, b, c) != (0, 0, 0)],
    key=lambda offset: -hops(offset),
)


def polynomial(square, coefficients):
    total = jnp.full_like(square, coefficients[-1])
    for coefficient in coefficients[-2::-1]:
        total = total * square + coefficient
    return total


def dot(a, b):
    return jnp.dot(a, b, preferred_element_type=F32)


def dot_nt(a, b):
    return lax.dot_general(a, b, (((1,), (1,)), ((), ())), preferred_element_type=F32)


def kernel(
    phase_hbm, dirty_hbm, pairs_hbm, live_hbm, out_ref,
    phase, dirty, pairs, live, cos_b, sin_b, points, esum, ediff,
    send_h, own_h, other_h, send_s, got_s, send_f, in_f, out_f, got_f, stack,
    rec_send, rec_got, sums_send, sums_got, part_send, part_got, count_send, count_got, count_f, count_b,
    eye_perm,
    load_sem, h_send, h_got, x_send, x_got, s_send, s_got, rec_ssem, rec_rsem, sum_ssem, sum_rsem,
    part_ssem, part_rsem, cnt_ssem, cnt_rsem,
):
    tiles, mics, width = phase.shape
    scale = float(mics * mics - mics)
    row, col = lax.axis_index("row"), lax.axis_index("col")
    x, core = lax.div(row, 2), lax.rem(row, 2)
    y, z = lax.div(col, 4), lax.rem(col, 4)
    me = col * 4 + x
    other = row + 1 - 2 * core

    barrier = pltpu.get_barrier_semaphore()

    def greet(px, pc, pcore):
        pl.semaphore_signal(
            barrier, inc=1, device_id=(px * 2 + pcore, pc), device_id_type=MESH
        )

    for offset in OFFSETS[:22]:
        px, pc = lax.rem(x + offset[0], 4), lax.rem(y + offset[1], 4) * 4 + lax.rem(z + offset[2], 4)
        greet(px, pc, core)

    loads = [
        pltpu.make_async_copy(phase_hbm.at[0], phase.at[0], load_sem.at[0]),
        pltpu.make_async_copy(phase_hbm.at[1], phase.at[1], load_sem.at[1]),
        pltpu.make_async_copy(dirty_hbm, dirty, load_sem.at[2]),
        pltpu.make_async_copy(pairs_hbm, pairs, load_sem.at[3]),
        pltpu.make_async_copy(live_hbm, live, load_sem.at[4]),
    ]
    for load in loads:
        load.start()

    for offset in OFFSETS[22:]:
        px, pc = lax.rem(x + offset[0], 4), lax.rem(y + offset[1], 4) * 4 + lax.rem(z + offset[2], 4)
        greet(px, pc, core)
    for da in range(4):
        greet(lax.rem(x + da, 4), col, 1 - core)

    lane = lax.broadcasted_iota(jnp.int32, (8, 128), 1)
    sub = lax.broadcasted_iota(jnp.int32, (8, 128), 0)
    chip_lane = col * 4 + x

    def sums_record(estimate):
        record = jnp.zeros((8, 128), F32)
        for t in range(tiles):
            total = jnp.sum(estimate[t : t + 1, :], axis=1, keepdims=True)
            record = jnp.where((sub == 4 + core) & (lane == t * 64 + chip_lane), total, record)
        return record

    def form(estimate):
        mats = []
        row_id = lax.broadcasted_iota(jnp.int32, (mics, mics), 0)
        col_id = lax.broadcasted_iota(jnp.int32, (mics, mics), 1)
        for t in range(tiles):
            value = estimate[t : t + 1, :]
            total = jnp.sum(value, axis=1, keepdims=True)
            left = jnp.concatenate(
                [(esum[t] * value).astype(BF), (ediff[t] * -value).astype(BF)], axis=1
            )
            mat = dot(left, points[t])
            mats.append(jnp.where(row_id == col_id, mat - total, mat))
        return mats

    upper = lax.broadcasted_iota(jnp.int32, (32, 8, 128), 1) < 4

    def cut_by_chip(mats):
        for half in range(2):
            parts = [m[:, half * 128 : half * 128 + 128].reshape(32, 8, 128) for m in mats]
            send_h[pl.ds(half * 32, 32)] = jnp.concatenate(parts, axis=1).astype(BF)

    def cut_by_core(mats):
        for half in range(2):
            first, second = [m[:, half * 128 : half * 128 + 128].reshape(32, 8, 128) for m in mats]
            second = pltpu.roll(second, 4, 1)
            send_f[pl.ds(half * 32, 32), 0] = jnp.where(upper, first, second).astype(BF)
            send_f[pl.ds(half * 32, 32), 1] = jnp.where(upper, second, first).astype(BF)

    def send_each(src, dst, ssem, rsem):
        for da, db, dc in OFFSETS + [(0, 0, 0)]:
            px = lax.rem(x + da, 4)
            pc = lax.rem(y + db, 4) * 4 + lax.rem(z + dc, 4)
            for apart in range(2):
                if (da, db, dc) != (0, 0, 0) or apart:
                    pcore = 1 - core if apart else core
                    pltpu.make_async_remote_copy(
                        src_ref=src(pc * 4 + px, pcore, apart), dst_ref=dst(apart),
                        send_sem=ssem, recv_sem=rsem,
                        device_id=(px * 2 + pcore, pc), device_id_type=MESH,
                    ).start()

    def send_all(src, dst, ssem, rsem):
        for da, db, dc in OFFSETS:
            px = lax.rem(x + da, 4)
            pc = lax.rem(y + db, 4) * 4 + lax.rem(z + dc, 4)
            pltpu.make_async_remote_copy(
                src_ref=src.at[pc * 4 + px], dst_ref=dst.at[me], send_sem=ssem, recv_sem=rsem,
                device_id=(px * 2 + core, pc), device_id_type=MESH,
            ).start()

    def send_row(src, dst, ssem, rsem):
        for k in (4, 5, 3, 2, 6, 7, 1):
            pltpu.make_async_remote_copy(
                src_ref=src, dst_ref=dst.at[row], send_sem=ssem, recv_sem=rsem,
                device_id=(lax.rem(row + k, 8), col), device_id_type=MESH,
            ).start()

    def send_col(src, dst, ssem, rsem):
        for da, db, dc in OFFSETS:
            if da == 0:
                pltpu.make_async_remote_copy(
                    src_ref=src, dst_ref=dst, send_sem=ssem, recv_sem=rsem,
                    device_id=(row, lax.rem(y + db, 4) * 4 + lax.rem(z + dc, 4)), device_id_type=MESH,
                ).start()

    def wait(ref, sem):
        pltpu.make_async_copy(ref, ref, sem).wait()

    loads[2].wait()
    powers, diags, firsts = [], [], []
    for t in range(tiles):
        loads[t].wait()
        angle = phase[t]
        square = angle * angle
        half_sine = polynomial(square, HALF_SIN) * angle
        twice = half_sine + half_sine
        cosine = (1.0 - twice * half_sine).astype(BF)
        sine = (twice * polynomial(square, HALF_COS)).astype(BF)
        cos_b[t] = cosine
        sin_b[t] = sine
        cosine, sine = cosine.astype(F32), sine.astype(F32)
        esum[t] = cosine + sine
        ediff[t] = cosine - sine
        power = jnp.sum(cosine * cosine + sine * sine, axis=0, keepdims=True)
        diag = (power * power - float(mics)) / scale
        powers.append(power)
        diags.append(diag)
        firsts.append(jnp.maximum(dirty[t : t + 1, :] / diag, 0.0))
        points[t] = jnp.concatenate([cosine.T, sine.T], axis=0).astype(BF)
    power = jnp.concatenate(powers, axis=0)
    diag = jnp.concatenate(diags, axis=0)
    estimate = jnp.concatenate(firsts, axis=0)

    loads[3].wait()
    loads[4].wait()
    slots = pairs.shape[1]
    first, second = pairs[0:1, :], pairs[1:2, :]
    first_lane = (first & 1) * 64 + ((first >> 1) & 15) * 4 + (first >> 6)
    second_row = (second >> 5) * 2 + (second & 1)
    listed = lax.broadcasted_iota(jnp.int32, (128, slots), 1) < live[0]
    first_hot = (lax.broadcasted_iota(jnp.int32, (128, slots), 0) == first_lane) & listed
    second_hot = lax.broadcasted_iota(jnp.int32, (16, slots), 0) == second_row
    part_send[...] = dot_nt(
        second_hot.astype(F32).astype(BF), first_hot.astype(F32).astype(BF)
    ).astype(BF)
    part_got[row] = part_send[...]
    record = sums_record(estimate)
    rec_send[0] = record
    rec_got[0, row] = record
    cut_by_chip(form(estimate))

    raw = lax.broadcasted_iota(jnp.int32, (256, 256), 1)
    raw_row = (raw >> 1) & 7
    placed = (((raw_row + core) & 1) << 7) + ((raw & 1) << 6) + ((raw >> 4) << 2) + (raw_row >> 1)
    eye_perm[...] = (lax.broadcasted_iota(jnp.int32, (256, 256), 0) == placed).astype(F32).astype(BF)

    pl.semaphore_wait(barrier, len(OFFSETS) + 4)

    for it in range(ITERS):
        if it == 0:
            send_row(part_send, part_got, part_ssem, part_rsem)
            send_all(send_h, own_h, h_send.at[0], h_got.at[0])
            own_h[me] = send_h[me]
            wait(part_got.at[pl.ds(0, 7)], part_rsem)
            by_core = [
                sum(part_got[2 * k + c].astype(F32) for k in range(4)).astype(BF) for c in range(2)
            ]
            count_send[:, 0:128] = jnp.where(core == 0, by_core[0], by_core[1])
            count_send[:, 128:256] = jnp.where(core == 0, by_core[1], by_core[0])
            here = pl.ds(pl.multiple_of(col * 16, 16), 16)
            count_got[here, :] = count_send[...]
            send_col(count_send, count_got.at[here], cnt_ssem, cnt_rsem)
            send_row(rec_send.at[0], rec_got.at[0], rec_ssem.at[0], rec_rsem.at[0])
            wait(own_h.at[pl.ds(0, 63)], h_got.at[0])
            exchange = pltpu.make_async_remote_copy(
                src_ref=own_h, dst_ref=other_h, send_sem=x_send, recv_sem=x_got,
                device_id=(other, col), device_id_type=MESH,
            )
            exchange.start()
        else:
            send_each(
                lambda slot, pcore, apart: send_f.at[slot, pcore],
                lambda apart: in_f.at[apart * 64 + me],
                h_send.at[it], h_got.at[it],
            )
            send_row(rec_send.at[it], rec_got.at[it], rec_ssem.at[it], rec_rsem.at[it])
            in_f[me] = send_f[me, core]

        wait(rec_got.at[it, pl.ds(0, 7)], rec_rsem.at[it])
        record = jnp.sum(rec_got[it], axis=0)
        sums_send[it] = record
        sums_got[it, col] = record
        send_col(sums_send.at[it], sums_got.at[it, col], sum_ssem.at[it], sum_rsem.at[it])

        if it == 0:
            for base, source in ((0, own_h), (128, other_h)):
                if base:
                    exchange.wait_recv()
                turned = jnp.swapaxes(source[...], 0, 1)
                for k in range(16):
                    stack[base + (k // 8) * 64 : base + (k // 8) * 64 + 64,
                          (k % 8) * 128 : (k % 8) * 128 + 128] = turned[k]
            wait(count_got.at[pl.ds(0, 240)], cnt_rsem)
            ordered = dot(eye_perm[...], count_got[...])
            here_id = lax.broadcasted_iota(jnp.int32, (128, 256), 0)
            all_id = lax.broadcasted_iota(jnp.int32, (128, 256), 1)
            counts = ordered[0:128, :] + ordered[:, 0:128].T + (here_id == all_id).astype(F32)
            count_f[...] = counts
            count_b[0:128, :] = counts.astype(BF)
            total = dot(count_b[0:128, :], stack[...])
            cut = [
                total[(k // 8) * 64 : (k // 8) * 64 + 64, (k % 8) * 128 : (k % 8) * 128 + 128]
                for k in range(16)
            ]
            send_s[...] = jnp.swapaxes(jnp.stack(cut, axis=0), 0, 1).astype(BF)
            send_all(send_s, got_s, s_send.at[0], s_got.at[0])
            got_s[me] = send_s[me]
            counts = ordered[128:256, :] + ordered[:, 128:256].T + (here_id + 128 == all_id).astype(F32)
            count_b[128:256, :] = counts.astype(BF)
        else:
            wait(in_f.at[pl.ds(0, 127)], h_got.at[it])
            turned = jnp.swapaxes(in_f[...], 0, 1)
            for k in range(4):
                first = jnp.where(core == 0, turned[k], turned[4 + k])
                second = jnp.where(core == 0, turned[4 + k], turned[k])
                for apart in range(2):
                    stack[apart * 128 : apart * 128 + 64, k * 128 : k * 128 + 128] = first[
                        apart * 64 : apart * 64 + 64
                    ]
                    stack[apart * 128 + 64 : apart * 128 + 128, k * 128 : k * 128 + 128] = second[
                        apart * 64 : apart * 64 + 64
                    ]
            total = dot(count_b[...], stack[:, 0:512])
            for apart in range(2):
                part = total[apart * 128 : apart * 128 + 128]
                top = jnp.where(core == 0, part[0:64], part[64:128])
                low = jnp.where(core == 0, part[64:128], part[0:64])
                cut = [v[:, k * 128 : k * 128 + 128] for v in (top, low) for k in range(4)]
                out_f[apart * 64 : apart * 64 + 64] = jnp.swapaxes(jnp.stack(cut, axis=0), 0, 1).astype(BF)
            send_each(
                lambda slot, pcore, apart: out_f.at[apart * 64 + slot],
                lambda apart: got_f.at[me * 2 + core],
                s_send.at[it], s_got.at[it],
            )
            got_f[me * 2 + core] = out_f[me]
        wait(sums_got.at[it, pl.ds(0, 15)], sum_rsem.at[it])
        sums = jnp.sum(sums_got[it], axis=0)
        own_sums = jnp.where(core == 0, sums[4:5, :], sums[5:6, :])
        other_sums = jnp.where(core == 0, sums[5:6, :], sums[4:5, :])
        partner = jnp.concatenate([own_sums, other_sums], axis=1)
        spread = [
            jnp.sum(count_f[pl.ds(t * 64 + chip_lane, 1), :] * partner, axis=1, keepdims=True)
            for t in range(tiles)
        ]

        if it == 0:
            wait(got_s.at[pl.ds(0, 63)], s_got.at[it])
        else:
            wait(got_f.at[pl.ds(0, 127)], s_got.at[it])
        news = []
        for t in range(tiles):
            halves = []
            for half in range(2):
                if it == 0:
                    block = got_s[half * 32 : half * 32 + 32].astype(F32)[:, t * 8 : t * 8 + 8, :]
                else:
                    pair = got_f[half * 64 : half * 64 + 64].astype(F32).reshape(32, 2, 8, 128)
                    block = jnp.where(upper, pair[:, t], pair[:, 1 - t])
                    if t:
                        block = pltpu.roll(block, 4, 1)
                halves.append(block.reshape(256, 128))
            mat = jnp.concatenate(halves, axis=1).astype(BF)
            form_sum = jnp.sum(
                esum[t] * dot(mat, cos_b[t]) - ediff[t] * dot(mat, sin_b[t]), axis=0, keepdims=True
            )
            value = (form_sum + spread[t] * (power[t : t + 1] - float(mics))) / scale
            old = estimate[t : t + 1]
            news.append(jnp.maximum(old + (dirty[t : t + 1, :] - value) / diag[t : t + 1], 0.0))
        estimate = jnp.concatenate(news, axis=0)
        if it + 1 < ITERS:
            record = sums_record(estimate)
            rec_send[it + 1] = record
            rec_got[it + 1, row] = record
            cut_by_core(form(estimate))

    out_ref[...] = estimate
    wait(send_h.at[pl.ds(0, 63)], h_send.at[0])
    wait(other_h, x_send)
    wait(send_s.at[pl.ds(0, 63)], s_send.at[0])
    wait(in_f.at[pl.ds(0, 127)], h_send.at[1])
    wait(out_f.at[pl.ds(0, 127)], s_send.at[1])
    for it in range(ITERS):
        wait(rec_got.at[it, pl.ds(0, 7)], rec_ssem.at[it])
        wait(sums_got.at[it, pl.ds(0, 15)], sum_ssem.at[it])
    wait(count_got.at[pl.ds(0, 240)], cnt_ssem)
    wait(part_got.at[pl.ds(0, 7)], part_ssem)


def on_device(phase, dirty_map, pairs, live):
    tiles, mics, width = phase.shape
    vmem, dma = pltpu.VMEM, pltpu.SemaphoreType.DMA
    blocks, fine = vmem((64, 16, 128), BF), vmem((128, 8, 128), BF)
    return pl.pallas_call(
        kernel,
        out_shape=jax.ShapeDtypeStruct(dirty_map.shape, F32),
        in_specs=[pl.BlockSpec(memory_space=pl.ANY)] * 4,
        out_specs=pl.BlockSpec(memory_space=pltpu.VMEM),
        scratch_shapes=[
            vmem((tiles, mics, width), F32),
            vmem((tiles, width), F32),
            vmem((2, pairs.shape[0]), jnp.int32),
            pltpu.SMEM((1,), jnp.int32),
            vmem((tiles, mics, width), BF),
            vmem((tiles, mics, width), BF),
            vmem((tiles, 2 * width, mics), BF),
            vmem((tiles, mics, width), F32),
            vmem((tiles, mics, width), F32),
            blocks, blocks, blocks, blocks, blocks,
            vmem((64, 2, 8, 128), BF), fine, fine, fine,
            vmem((256, 1024), BF),
            vmem((ITERS, 8, 128), F32),
            vmem((ITERS, 8, 8, 128), F32),
            vmem((ITERS, 8, 128), F32),
            vmem((ITERS, 16, 8, 128), F32),
            vmem((16, 128), BF),
            vmem((8, 16, 128), BF),
            vmem((16, 256), BF),
            vmem((256, 256), BF),
            vmem((128, 256), F32),
            vmem((256, 256), BF),
            vmem((256, 256), BF),
            dma((5,)),
            dma((ITERS,)), dma((ITERS,)), dma, dma, dma((ITERS,)), dma((ITERS,)),
            dma((ITERS,)), dma((ITERS,)), dma((ITERS,)), dma((ITERS,)),
            dma, dma, dma, dma,
        ],
        compiler_params=pltpu.CompilerParams(
            collective_id=0, has_side_effects=True, vmem_limit_bytes=48 << 20
        ),
    )(*[pltpu.with_memory_space_constraint(v, pltpu.HBM) for v in (phase, dirty_map, pairs.T)], live)


def solution(mesh):
    in_specs = (
        P(("row", "col"), None, None),
        P(("row", "col"), None),
        P(("row", "col"), None),
        P(("row", "col")),
    )
    out_specs = P(("row", "col"), None)
    return jax.shard_map(
        on_device, mesh=mesh, in_specs=in_specs, out_specs=out_specs, check_vma=False
    )
```

```python
import functools

import jax
import jax.numpy as jnp
from jax import lax
from jax.experimental import pallas as pl
from jax.experimental.pallas import tpu as pltpu
from jax.sharding import PartitionSpec as P

ITERS = 2
MESH = pl.DeviceIdType.MESH
BF = jnp.bfloat16
F32 = jnp.float32
HALF_COS = (0.9999999403953552, -0.1249997615814209, 0.002603973960503936, -2.1646421373588964e-05,
            9.044592985674171e-08)
HALF_SIN = (0.5, -0.020833322778344154, 0.0002604078617878258, -1.5475848158530425e-06,
            5.0883919300304115e-09)


def hops(offset):
    return sum(min(step, 4 - step) for step in offset)


OFFSETS = sorted(
    [(a, b, c) for a in range(4) for b in range(4) for c in range(4) if (a, b, c) != (0, 0, 0)],
    key=lambda offset: -hops(offset),
)


def polynomial(square, coefficients):
    total = jnp.full_like(square, coefficients[-1])
    for coefficient in coefficients[-2::-1]:
        total = total * square + coefficient
    return total


def dot(a, b):
    return jnp.dot(a, b, preferred_element_type=F32)


def dot_nt(a, b):
    return lax.dot_general(a, b, (((1,), (1,)), ((), ())), preferred_element_type=F32)


def kernel(
    phase_hbm, dirty_hbm, pairs_hbm, live_hbm, out_ref,
    phase, dirty, pairs, live, cos_b, sin_b, points, esum, ediff,
    send_h, own_h, other_h, send_s, got_s, send_f, in_f, out_f, got_f, stack,
    rec_send, rec_got, sums_send, sums_got, part_send, part_got, count_send, count_got, count_f, count_b,
    eye_perm,
    load_sem, h_send, h_got, x_send, x_got, s_send, s_got, rec_ssem, rec_rsem, sum_ssem, sum_rsem,
    part_ssem, part_rsem, cnt_ssem, cnt_rsem,
):
    tiles, mics, width = phase.shape
    scale = float(mics * mics - mics)
    row, col = lax.axis_index("row"), lax.axis_index("col")
    x, core = lax.div(row, 2), lax.rem(row, 2)
    y, z = lax.div(col, 4), lax.rem(col, 4)
    me = col * 4 + x
    other = row + 1 - 2 * core

    barrier = pltpu.get_barrier_semaphore()

    def greet(px, pc, pcore):
        pl.semaphore_signal(
            barrier, inc=1, device_id=(px * 2 + pcore, pc), device_id_type=MESH
        )

    for offset in OFFSETS[:22]:
        px, pc = lax.rem(x + offset[0], 4), lax.rem(y + offset[1], 4) * 4 + lax.rem(z + offset[2], 4)
        greet(px, pc, core)

    loads = [
        pltpu.make_async_copy(phase_hbm.at[0], phase.at[0], load_sem.at[0]),
        pltpu.make_async_copy(phase_hbm.at[1], phase.at[1], load_sem.at[1]),
        pltpu.make_async_copy(dirty_hbm, dirty, load_sem.at[2]),
        pltpu.make_async_copy(pairs_hbm, pairs, load_sem.at[3]),
        pltpu.make_async_copy(live_hbm, live, load_sem.at[4]),
    ]
    for load in loads:
        load.start()

    for offset in OFFSETS[22:]:
        px, pc = lax.rem(x + offset[0], 4), lax.rem(y + offset[1], 4) * 4 + lax.rem(z + offset[2], 4)
        greet(px, pc, core)
    for da in range(4):
        greet(lax.rem(x + da, 4), col, 1 - core)

    lane = lax.broadcasted_iota(jnp.int32, (8, 128), 1)
    sub = lax.broadcasted_iota(jnp.int32, (8, 128), 0)
    chip_lane = col * 4 + x

    def sums_record(estimate):
        record = jnp.zeros((8, 128), F32)
        for t in range(tiles):
            total = jnp.sum(estimate[t : t + 1, :], axis=1, keepdims=True)
            record = jnp.where((sub == 4 + core) & (lane == t * 64 + chip_lane), total, record)
        return record

    def form(estimate):
        mats = []
        row_id = lax.broadcasted_iota(jnp.int32, (mics, mics), 0)
        col_id = lax.broadcasted_iota(jnp.int32, (mics, mics), 1)
        for t in range(tiles):
            value = estimate[t : t + 1, :]
            total = jnp.sum(value, axis=1, keepdims=True)
            left = jnp.concatenate(
                [(esum[t] * value).astype(BF), (ediff[t] * -value).astype(BF)], axis=1
            )
            mat = dot(left, points[t])
            mats.append(jnp.where(row_id == col_id, mat - total, mat))
        return mats

    upper = lax.broadcasted_iota(jnp.int32, (32, 8, 128), 1) < 4

    def cut_by_chip(mats):
        for half in range(2):
            parts = [m[:, half * 128 : half * 128 + 128].reshape(32, 8, 128) for m in mats]
            send_h[pl.ds(half * 32, 32)] = jnp.concatenate(parts, axis=1).astype(BF)

    def cut_by_core(mats):
        for half in range(2):
            first, second = [m[:, half * 128 : half * 128 + 128].reshape(32, 8, 128) for m in mats]
            second = pltpu.roll(second, 4, 1)
            send_f[pl.ds(half * 32, 32), 0] = jnp.where(upper, first, second).astype(BF)
            send_f[pl.ds(half * 32, 32), 1] = jnp.where(upper, second, first).astype(BF)

    def send_each(src, dst, ssem, rsem, lead=False):
        targets = []
        for da, db, dc in OFFSETS + [(0, 0, 0)]:
            px = lax.rem(x + da, 4)
            pc = lax.rem(y + db, 4) * 4 + lax.rem(z + dc, 4)
            for apart in range(2):
                if (da, db, dc) != (0, 0, 0) or apart:
                    targets.append((px * 2 + (1 - core if apart else core), pc))
        if lead:
            first_row, first_col = targets[0]
            mine = (row == 1) & (col == 0)
            moved = [(jnp.where(mine, first_row, 1), jnp.where(mine, first_col, 0))]
            for prow, pcol in targets[1:]:
                hit = (prow == 1) & (pcol == 0)
                moved.append((jnp.where(hit, first_row, prow), jnp.where(hit, first_col, pcol)))
            targets = moved
        for prow, pcol in targets:
            slot, pcore = pcol * 4 + lax.div(prow, 2), lax.rem(prow, 2)
            apart = lax.rem(core + pcore, 2)
            pltpu.make_async_remote_copy(
                src_ref=src(slot, pcore, apart), dst_ref=dst(apart), send_sem=ssem, recv_sem=rsem,
                device_id=(prow, pcol), device_id_type=MESH,
            ).start()

    def send_all(src, dst, ssem, rsem):
        for da, db, dc in OFFSETS:
            px = lax.rem(x + da, 4)
            pc = lax.rem(y + db, 4) * 4 + lax.rem(z + dc, 4)
            pltpu.make_async_remote_copy(
                src_ref=src.at[pc * 4 + px], dst_ref=dst.at[me], send_sem=ssem, recv_sem=rsem,
                device_id=(px * 2 + core, pc), device_id_type=MESH,
            ).start()

    def send_row(src, dst, ssem, rsem):
        for k in (4, 5, 3, 2, 6, 7, 1):
            pltpu.make_async_remote_copy(
                src_ref=src, dst_ref=dst.at[row], send_sem=ssem, recv_sem=rsem,
                device_id=(lax.rem(row + k, 8), col), device_id_type=MESH,
            ).start()

    def send_col(src, dst, ssem, rsem):
        for da, db, dc in OFFSETS:
            if da == 0:
                pltpu.make_async_remote_copy(
                    src_ref=src, dst_ref=dst, send_sem=ssem, recv_sem=rsem,
                    device_id=(row, lax.rem(y + db, 4) * 4 + lax.rem(z + dc, 4)), device_id_type=MESH,
                ).start()

    def wait(ref, sem):
        pltpu.make_async_copy(ref, ref, sem).wait()

    loads[2].wait()
    powers, diags, firsts = [], [], []
    for t in range(tiles):
        loads[t].wait()
        angle = phase[t]
        square = angle * angle
        half_sine = polynomial(square, HALF_SIN) * angle
        twice = half_sine + half_sine
        cosine = (1.0 - twice * half_sine).astype(BF)
        sine = (twice * polynomial(square, HALF_COS)).astype(BF)
        cos_b[t] = cosine
        sin_b[t] = sine
        cosine, sine = cosine.astype(F32), sine.astype(F32)
        esum[t] = cosine + sine
        ediff[t] = cosine - sine
        power = jnp.sum(cosine * cosine + sine * sine, axis=0, keepdims=True)
        diag = (power * power - float(mics)) / scale
        powers.append(power)
        diags.append(diag)
        firsts.append(jnp.maximum(dirty[t : t + 1, :] / diag, 0.0))
        points[t] = jnp.concatenate([cosine.T, sine.T], axis=0).astype(BF)
    power = jnp.concatenate(powers, axis=0)
    diag = jnp.concatenate(diags, axis=0)
    estimate = jnp.concatenate(firsts, axis=0)

    loads[3].wait()
    loads[4].wait()
    slots = pairs.shape[1]
    first, second = pairs[0:1, :], pairs[1:2, :]
    first_lane = (first & 1) * 64 + ((first >> 1) & 15) * 4 + (first >> 6)
    second_row = (second >> 5) * 2 + (second & 1)
    listed = lax.broadcasted_iota(jnp.int32, (128, slots), 1) < live[0]
    first_hot = (lax.broadcasted_iota(jnp.int32, (128, slots), 0) == first_lane) & listed
    second_hot = lax.broadcasted_iota(jnp.int32, (16, slots), 0) == second_row
    part_send[...] = dot_nt(
        second_hot.astype(F32).astype(BF), first_hot.astype(F32).astype(BF)
    ).astype(BF)
    part_got[row] = part_send[...]
    record = sums_record(estimate)
    rec_send[0] = record
    rec_got[0, row] = record
    cut_by_chip(form(estimate))

    raw = lax.broadcasted_iota(jnp.int32, (256, 256), 1)
    raw_row = (raw >> 1) & 7
    placed = (((raw_row + core) & 1) << 7) + ((raw & 1) << 6) + ((raw >> 4) << 2) + (raw_row >> 1)
    eye_perm[...] = (lax.broadcasted_iota(jnp.int32, (256, 256), 0) == placed).astype(F32).astype(BF)

    pl.semaphore_wait(barrier, len(OFFSETS) + 4)

    for it in range(ITERS):
        if it == 0:
            send_row(part_send, part_got, part_ssem, part_rsem)
            send_all(send_h, own_h, h_send.at[0], h_got.at[0])
            own_h[me] = send_h[me]
            wait(part_got.at[pl.ds(0, 7)], part_rsem)
            by_core = [
                sum(part_got[2 * k + c].astype(F32) for k in range(4)).astype(BF) for c in range(2)
            ]
            count_send[:, 0:128] = jnp.where(core == 0, by_core[0], by_core[1])
            count_send[:, 128:256] = jnp.where(core == 0, by_core[1], by_core[0])
            here = pl.ds(pl.multiple_of(col * 16, 16), 16)
            count_got[here, :] = count_send[...]
            send_col(count_send, count_got.at[here], cnt_ssem, cnt_rsem)
            send_row(rec_send.at[0], rec_got.at[0], rec_ssem.at[0], rec_rsem.at[0])
            wait(own_h.at[pl.ds(0, 63)], h_got.at[0])
            exchange = pltpu.make_async_remote_copy(
                src_ref=own_h, dst_ref=other_h, send_sem=x_send, recv_sem=x_got,
                device_id=(other, col), device_id_type=MESH,
            )
            exchange.start()
        else:
            send_each(
                lambda slot, pcore, apart: send_f.at[slot, pcore],
                lambda apart: in_f.at[apart * 64 + me],
                h_send.at[it], h_got.at[it],
            )
            send_row(rec_send.at[it], rec_got.at[it], rec_ssem.at[it], rec_rsem.at[it])
            in_f[me] = send_f[me, core]

        wait(rec_got.at[it, pl.ds(0, 7)], rec_rsem.at[it])
        record = jnp.sum(rec_got[it], axis=0)
        sums_send[it] = record
        sums_got[it, col] = record
        send_col(sums_send.at[it], sums_got.at[it, col], sum_ssem.at[it], sum_rsem.at[it])

        if it == 0:
            for base, source in ((0, own_h), (128, other_h)):
                if base:
                    exchange.wait_recv()
                turned = jnp.swapaxes(source[...], 0, 1)
                for k in range(16):
                    stack[base + (k // 8) * 64 : base + (k // 8) * 64 + 64,
                          (k % 8) * 128 : (k % 8) * 128 + 128] = turned[k]
            wait(count_got.at[pl.ds(0, 240)], cnt_rsem)
            ordered = dot(eye_perm[...], count_got[...])
            here_id = lax.broadcasted_iota(jnp.int32, (128, 256), 0)
            all_id = lax.broadcasted_iota(jnp.int32, (128, 256), 1)
            counts = ordered[0:128, :] + ordered[:, 0:128].T + (here_id == all_id).astype(F32)
            count_f[...] = counts
            count_b[0:128, :] = counts.astype(BF)
            total = dot(count_b[0:128, :], stack[...])
            cut = [
                total[(k // 8) * 64 : (k // 8) * 64 + 64, (k % 8) * 128 : (k % 8) * 128 + 128]
                for k in range(16)
            ]
            send_s[...] = jnp.swapaxes(jnp.stack(cut, axis=0), 0, 1).astype(BF)
            send_all(send_s, got_s, s_send.at[0], s_got.at[0])
            got_s[me] = send_s[me]
            counts = ordered[128:256, :] + ordered[:, 128:256].T + (here_id + 128 == all_id).astype(F32)
            count_b[128:256, :] = counts.astype(BF)
        else:
            wait(in_f.at[pl.ds(0, 127)], h_got.at[it])
            turned = jnp.swapaxes(in_f[...], 0, 1)
            for k in range(4):
                first = jnp.where(core == 0, turned[k], turned[4 + k])
                second = jnp.where(core == 0, turned[4 + k], turned[k])
                for apart in range(2):
                    stack[apart * 128 : apart * 128 + 64, k * 128 : k * 128 + 128] = first[
                        apart * 64 : apart * 64 + 64
                    ]
                    stack[apart * 128 + 64 : apart * 128 + 128, k * 128 : k * 128 + 128] = second[
                        apart * 64 : apart * 64 + 64
                    ]
            total = dot(count_b[...], stack[:, 0:512])
            for apart in range(2):
                part = total[apart * 128 : apart * 128 + 128]
                top = jnp.where(core == 0, part[0:64], part[64:128])
                low = jnp.where(core == 0, part[64:128], part[0:64])
                cut = [v[:, k * 128 : k * 128 + 128] for v in (top, low) for k in range(4)]
                out_f[apart * 64 : apart * 64 + 64] = jnp.swapaxes(jnp.stack(cut, axis=0), 0, 1).astype(BF)
            send_each(
                lambda slot, pcore, apart: out_f.at[apart * 64 + slot],
                lambda apart: got_f.at[me * 2 + core],
                s_send.at[it], s_got.at[it], lead=True,
            )
            got_f[me * 2 + core] = out_f[me]
        wait(sums_got.at[it, pl.ds(0, 15)], sum_rsem.at[it])
        sums = jnp.sum(sums_got[it], axis=0)
        own_sums = jnp.where(core == 0, sums[4:5, :], sums[5:6, :])
        other_sums = jnp.where(core == 0, sums[5:6, :], sums[4:5, :])
        partner = jnp.concatenate([own_sums, other_sums], axis=1)
        spread = [
            jnp.sum(count_f[pl.ds(t * 64 + chip_lane, 1), :] * partner, axis=1, keepdims=True)
            for t in range(tiles)
        ]

        if it == 0:
            wait(got_s.at[pl.ds(0, 63)], s_got.at[it])
        else:
            wait(got_f.at[pl.ds(0, 127)], s_got.at[it])
        news = []
        for t in range(tiles):
            halves = []
            for half in range(2):
                if it == 0:
                    block = got_s[half * 32 : half * 32 + 32].astype(F32)[:, t * 8 : t * 8 + 8, :]
                else:
                    pair = got_f[half * 64 : half * 64 + 64].astype(F32).reshape(32, 2, 8, 128)
                    block = jnp.where(upper, pair[:, t], pair[:, 1 - t])
                    if t:
                        block = pltpu.roll(block, 4, 1)
                halves.append(block.reshape(256, 128))
            mat = jnp.concatenate(halves, axis=1).astype(BF)
            form_sum = jnp.sum(
                esum[t] * dot(mat, cos_b[t]) - ediff[t] * dot(mat, sin_b[t]), axis=0, keepdims=True
            )
            value = (form_sum + spread[t] * (power[t : t + 1] - float(mics))) / scale
            old = estimate[t : t + 1]
            news.append(jnp.maximum(old + (dirty[t : t + 1, :] - value) / diag[t : t + 1], 0.0))
        estimate = jnp.concatenate(news, axis=0)
        if it + 1 < ITERS:
            record = sums_record(estimate)
            rec_send[it + 1] = record
            rec_got[it + 1, row] = record
            cut_by_core(form(estimate))

    out_ref[...] = estimate
    wait(send_h.at[pl.ds(0, 63)], h_send.at[0])
    wait(other_h, x_send)
    wait(send_s.at[pl.ds(0, 63)], s_send.at[0])
    wait(in_f.at[pl.ds(0, 127)], h_send.at[1])
    wait(out_f.at[pl.ds(0, 127)], s_send.at[1])
    for it in range(ITERS):
        wait(rec_got.at[it, pl.ds(0, 7)], rec_ssem.at[it])
        wait(sums_got.at[it, pl.ds(0, 15)], sum_ssem.at[it])
    wait(count_got.at[pl.ds(0, 240)], cnt_ssem)
    wait(part_got.at[pl.ds(0, 7)], part_ssem)


def on_device(phase, dirty_map, pairs, live):
    tiles, mics, width = phase.shape
    vmem, dma = pltpu.VMEM, pltpu.SemaphoreType.DMA
    blocks, fine = vmem((64, 16, 128), BF), vmem((128, 8, 128), BF)
    return pl.pallas_call(
        kernel,
        out_shape=jax.ShapeDtypeStruct(dirty_map.shape, F32),
        in_specs=[pl.BlockSpec(memory_space=pl.ANY)] * 4,
        out_specs=pl.BlockSpec(memory_space=pltpu.VMEM),
        scratch_shapes=[
            vmem((tiles, mics, width), F32),
            vmem((tiles, width), F32),
            vmem((2, pairs.shape[0]), jnp.int32),
            pltpu.SMEM((1,), jnp.int32),
            vmem((tiles, mics, width), BF),
            vmem((tiles, mics, width), BF),
            vmem((tiles, 2 * width, mics), BF),
            vmem((tiles, mics, width), F32),
            vmem((tiles, mics, width), F32),
            blocks, blocks, blocks, blocks, blocks,
            vmem((64, 2, 8, 128), BF), fine, fine, fine,
            vmem((256, 1024), BF),
            vmem((ITERS, 8, 128), F32),
            vmem((ITERS, 8, 8, 128), F32),
            vmem((ITERS, 8, 128), F32),
            vmem((ITERS, 16, 8, 128), F32),
            vmem((16, 128), BF),
            vmem((8, 16, 128), BF),
            vmem((16, 256), BF),
            vmem((256, 256), BF),
            vmem((128, 256), F32),
            vmem((256, 256), BF),
            vmem((256, 256), BF),
            dma((5,)),
            dma((ITERS,)), dma((ITERS,)), dma, dma, dma((ITERS,)), dma((ITERS,)),
            dma((ITERS,)), dma((ITERS,)), dma((ITERS,)), dma((ITERS,)),
            dma, dma, dma, dma,
        ],
        compiler_params=pltpu.CompilerParams(
            collective_id=0, has_side_effects=True, vmem_limit_bytes=48 << 20
        ),
    )(*[pltpu.with_memory_space_constraint(v, pltpu.HBM) for v in (phase, dirty_map, pairs.T)], live)


def solution(mesh):
    in_specs = (
        P(("row", "col"), None, None),
        P(("row", "col"), None),
        P(("row", "col"), None),
        P(("row", "col")),
    )
    out_specs = P(("row", "col"), None)
    return jax.shard_map(
        on_device, mesh=mesh, in_specs=in_specs, out_specs=out_specs, check_vma=False
    )
```

```python
import functools

import jax
import jax.numpy as jnp
from jax import lax
from jax.experimental import pallas as pl
from jax.experimental.pallas import tpu as pltpu
from jax.sharding import PartitionSpec as P

ITERS = 2
LEAD = (1, 0)
MESH = pl.DeviceIdType.MESH
BF = jnp.bfloat16
F32 = jnp.float32
HALF_COS = (0.9999999403953552, -0.1249997615814209, 0.002603973960503936, -2.1646421373588964e-05,
            9.044592985674171e-08)
HALF_SIN = (0.5, -0.020833322778344154, 0.0002604078617878258, -1.5475848158530425e-06,
            5.0883919300304115e-09)


def hops(offset):
    return sum(min(step, 4 - step) for step in offset)


OFFSETS = sorted(
    [(a, b, c) for a in range(4) for b in range(4) for c in range(4) if (a, b, c) != (0, 0, 0)],
    key=lambda offset: -hops(offset),
)


def polynomial(square, coefficients):
    total = jnp.full_like(square, coefficients[-1])
    for coefficient in coefficients[-2::-1]:
        total = total * square + coefficient
    return total


def dot(a, b):
    return jnp.dot(a, b, preferred_element_type=F32)


def dot_nt(a, b):
    return lax.dot_general(a, b, (((1,), (1,)), ((), ())), preferred_element_type=F32)


def kernel(
    phase_hbm, dirty_hbm, pairs_hbm, live_hbm, out_ref,
    phase, dirty, pairs, live, cos_b, sin_b, points, esum, ediff,
    send_h, own_h, other_h, send_s, got_s, send_f, in_f, out_f, got_f, stack,
    rec_send, rec_got, sums_send, sums_got, part_send, part_got, count_send, count_got, count_f, count_b,
    eye_perm,
    load_sem, h_send, h_got, x_send, x_got, s_send, s_got, rec_ssem, rec_rsem, sum_ssem, sum_rsem,
    part_ssem, part_rsem, cnt_ssem, cnt_rsem,
):
    tiles, mics, width = phase.shape
    scale = float(mics * mics - mics)
    row, col = lax.axis_index("row"), lax.axis_index("col")
    x, core = lax.div(row, 2), lax.rem(row, 2)
    y, z = lax.div(col, 4), lax.rem(col, 4)
    me = col * 4 + x
    other = row + 1 - 2 * core

    barrier = pltpu.get_barrier_semaphore()

    def greet(px, pc, pcore):
        pl.semaphore_signal(
            barrier, inc=1, device_id=(px * 2 + pcore, pc), device_id_type=MESH
        )

    for offset in OFFSETS[:22]:
        px, pc = lax.rem(x + offset[0], 4), lax.rem(y + offset[1], 4) * 4 + lax.rem(z + offset[2], 4)
        greet(px, pc, core)

    loads = [
        pltpu.make_async_copy(phase_hbm.at[0], phase.at[0], load_sem.at[0]),
        pltpu.make_async_copy(phase_hbm.at[1], phase.at[1], load_sem.at[1]),
        pltpu.make_async_copy(dirty_hbm, dirty, load_sem.at[2]),
        pltpu.make_async_copy(pairs_hbm, pairs, load_sem.at[3]),
        pltpu.make_async_copy(live_hbm, live, load_sem.at[4]),
    ]
    for load in loads:
        load.start()

    for offset in OFFSETS[22:]:
        px, pc = lax.rem(x + offset[0], 4), lax.rem(y + offset[1], 4) * 4 + lax.rem(z + offset[2], 4)
        greet(px, pc, core)
    for da in range(4):
        greet(lax.rem(x + da, 4), col, 1 - core)

    lane = lax.broadcasted_iota(jnp.int32, (8, 128), 1)
    sub = lax.broadcasted_iota(jnp.int32, (8, 128), 0)
    chip_lane = col * 4 + x

    def sums_record(estimate):
        record = jnp.zeros((8, 128), F32)
        for t in range(tiles):
            total = jnp.sum(estimate[t : t + 1, :], axis=1, keepdims=True)
            record = jnp.where((sub == 4 + core) & (lane == t * 64 + chip_lane), total, record)
        return record

    def form(estimate):
        mats = []
        row_id = lax.broadcasted_iota(jnp.int32, (mics, mics), 0)
        col_id = lax.broadcasted_iota(jnp.int32, (mics, mics), 1)
        for t in range(tiles):
            value = estimate[t : t + 1, :]
            total = jnp.sum(value, axis=1, keepdims=True)
            left = jnp.concatenate(
                [(esum[t] * value).astype(BF), (ediff[t] * -value).astype(BF)], axis=1
            )
            mat = dot(left, points[t])
            mats.append(jnp.where(row_id == col_id, mat - total, mat))
        return mats

    upper = lax.broadcasted_iota(jnp.int32, (32, 8, 128), 1) < 4

    def cut_by_chip(mats):
        for half in range(2):
            parts = [m[:, half * 128 : half * 128 + 128].reshape(32, 8, 128) for m in mats]
            send_h[pl.ds(half * 32, 32)] = jnp.concatenate(parts, axis=1).astype(BF)

    def cut_by_core(mats):
        for half in range(2):
            first, second = [m[:, half * 128 : half * 128 + 128].reshape(32, 8, 128) for m in mats]
            second = pltpu.roll(second, 4, 1)
            send_f[pl.ds(half * 32, 32), 0] = jnp.where(upper, first, second).astype(BF)
            send_f[pl.ds(half * 32, 32), 1] = jnp.where(upper, second, first).astype(BF)

    def send_each(src, dst, ssem, rsem, lead=False):
        targets = []
        for da, db, dc in OFFSETS + [(0, 0, 0)]:
            px = lax.rem(x + da, 4)
            pc = lax.rem(y + db, 4) * 4 + lax.rem(z + dc, 4)
            for apart in range(2):
                if (da, db, dc) != (0, 0, 0) or apart:
                    targets.append((px * 2 + (1 - core if apart else core), pc))
        for place, ahead in enumerate(LEAD if lead else ()):
            first_row, first_col = targets[place]
            mine = (row == ahead) & (col == 0)
            moved = [(jnp.where(mine, first_row, ahead), jnp.where(mine, first_col, 0))]
            for prow, pcol in targets[place + 1 :]:
                hit = (prow == ahead) & (pcol == 0)
                moved.append((jnp.where(hit, first_row, prow), jnp.where(hit, first_col, pcol)))
            targets = targets[:place] + moved
        for prow, pcol in targets:
            slot, pcore = pcol * 4 + lax.div(prow, 2), lax.rem(prow, 2)
            apart = lax.rem(core + pcore, 2)
            pltpu.make_async_remote_copy(
                src_ref=src(slot, pcore, apart), dst_ref=dst(apart), send_sem=ssem, recv_sem=rsem,
                device_id=(prow, pcol), device_id_type=MESH,
            ).start()

    def send_all(src, dst, ssem, rsem):
        for da, db, dc in OFFSETS:
            px = lax.rem(x + da, 4)
            pc = lax.rem(y + db, 4) * 4 + lax.rem(z + dc, 4)
            pltpu.make_async_remote_copy(
                src_ref=src.at[pc * 4 + px], dst_ref=dst.at[me], send_sem=ssem, recv_sem=rsem,
                device_id=(px * 2 + core, pc), device_id_type=MESH,
            ).start()

    def send_row(src, dst, ssem, rsem):
        for k in (4, 5, 3, 2, 6, 7, 1):
            pltpu.make_async_remote_copy(
                src_ref=src, dst_ref=dst.at[row], send_sem=ssem, recv_sem=rsem,
                device_id=(lax.rem(row + k, 8), col), device_id_type=MESH,
            ).start()

    def send_col(src, dst, ssem, rsem):
        for da, db, dc in OFFSETS:
            if da == 0:
                pltpu.make_async_remote_copy(
                    src_ref=src, dst_ref=dst, send_sem=ssem, recv_sem=rsem,
                    device_id=(row, lax.rem(y + db, 4) * 4 + lax.rem(z + dc, 4)), device_id_type=MESH,
                ).start()

    def wait(ref, sem):
        pltpu.make_async_copy(ref, ref, sem).wait()

    loads[2].wait()
    powers, diags, firsts = [], [], []
    for t in range(tiles):
        loads[t].wait()
        angle = phase[t]
        square = angle * angle
        half_sine = polynomial(square, HALF_SIN) * angle
        twice = half_sine + half_sine
        cosine = (1.0 - twice * half_sine).astype(BF)
        sine = (twice * polynomial(square, HALF_COS)).astype(BF)
        cos_b[t] = cosine
        sin_b[t] = sine
        cosine, sine = cosine.astype(F32), sine.astype(F32)
        esum[t] = cosine + sine
        ediff[t] = cosine - sine
        power = jnp.sum(cosine * cosine + sine * sine, axis=0, keepdims=True)
        diag = (power * power - float(mics)) / scale
        powers.append(power)
        diags.append(diag)
        firsts.append(jnp.maximum(dirty[t : t + 1, :] / diag, 0.0))
        points[t] = jnp.concatenate([cosine.T, sine.T], axis=0).astype(BF)
    power = jnp.concatenate(powers, axis=0)
    diag = jnp.concatenate(diags, axis=0)
    estimate = jnp.concatenate(firsts, axis=0)

    loads[3].wait()
    loads[4].wait()
    slots = pairs.shape[1]
    first, second = pairs[0:1, :], pairs[1:2, :]
    first_lane = (first & 1) * 64 + ((first >> 1) & 15) * 4 + (first >> 6)
    second_row = (second >> 5) * 2 + (second & 1)
    listed = lax.broadcasted_iota(jnp.int32, (128, slots), 1) < live[0]
    first_hot = (lax.broadcasted_iota(jnp.int32, (128, slots), 0) == first_lane) & listed
    second_hot = lax.broadcasted_iota(jnp.int32, (16, slots), 0) == second_row
    part_send[...] = dot_nt(
        second_hot.astype(F32).astype(BF), first_hot.astype(F32).astype(BF)
    ).astype(BF)
    part_got[row] = part_send[...]
    record = sums_record(estimate)
    rec_send[0] = record
    rec_got[0, row] = record
    cut_by_chip(form(estimate))

    raw = lax.broadcasted_iota(jnp.int32, (256, 256), 1)
    raw_row = (raw >> 1) & 7
    placed = (((raw_row + core) & 1) << 7) + ((raw & 1) << 6) + ((raw >> 4) << 2) + (raw_row >> 1)
    eye_perm[...] = (lax.broadcasted_iota(jnp.int32, (256, 256), 0) == placed).astype(F32).astype(BF)

    pl.semaphore_wait(barrier, len(OFFSETS) + 4)

    for it in range(ITERS):
        if it == 0:
            send_row(part_send, part_got, part_ssem, part_rsem)
            send_all(send_h, own_h, h_send.at[0], h_got.at[0])
            own_h[me] = send_h[me]
            wait(part_got.at[pl.ds(0, 7)], part_rsem)
            by_core = [
                sum(part_got[2 * k + c].astype(F32) for k in range(4)).astype(BF) for c in range(2)
            ]
            count_send[:, 0:128] = jnp.where(core == 0, by_core[0], by_core[1])
            count_send[:, 128:256] = jnp.where(core == 0, by_core[1], by_core[0])
            here = pl.ds(pl.multiple_of(col * 16, 16), 16)
            count_got[here, :] = count_send[...]
            send_col(count_send, count_got.at[here], cnt_ssem, cnt_rsem)
            send_row(rec_send.at[0], rec_got.at[0], rec_ssem.at[0], rec_rsem.at[0])
            wait(own_h.at[pl.ds(0, 63)], h_got.at[0])
            exchange = pltpu.make_async_remote_copy(
                src_ref=own_h, dst_ref=other_h, send_sem=x_send, recv_sem=x_got,
                device_id=(other, col), device_id_type=MESH,
            )
            exchange.start()
        else:
            send_each(
                lambda slot, pcore, apart: send_f.at[slot, pcore],
                lambda apart: in_f.at[apart * 64 + me],
                h_send.at[it], h_got.at[it],
            )
            send_row(rec_send.at[it], rec_got.at[it], rec_ssem.at[it], rec_rsem.at[it])
            in_f[me] = send_f[me, core]

        wait(rec_got.at[it, pl.ds(0, 7)], rec_rsem.at[it])
        record = jnp.sum(rec_got[it], axis=0)
        sums_send[it] = record
        sums_got[it, col] = record
        send_col(sums_send.at[it], sums_got.at[it, col], sum_ssem.at[it], sum_rsem.at[it])

        if it == 0:
            for base, source in ((0, own_h), (128, other_h)):
                if base:
                    exchange.wait_recv()
                turned = jnp.swapaxes(source[...], 0, 1)
                for k in range(16):
                    stack[base + (k // 8) * 64 : base + (k // 8) * 64 + 64,
                          (k % 8) * 128 : (k % 8) * 128 + 128] = turned[k]
            wait(count_got.at[pl.ds(0, 240)], cnt_rsem)
            ordered = dot(eye_perm[...], count_got[...])
            here_id = lax.broadcasted_iota(jnp.int32, (128, 256), 0)
            all_id = lax.broadcasted_iota(jnp.int32, (128, 256), 1)
            counts = ordered[0:128, :] + ordered[:, 0:128].T + (here_id == all_id).astype(F32)
            count_f[...] = counts
            count_b[0:128, :] = counts.astype(BF)
            total = dot(count_b[0:128, :], stack[...])
            cut = [
                total[(k // 8) * 64 : (k // 8) * 64 + 64, (k % 8) * 128 : (k % 8) * 128 + 128]
                for k in range(16)
            ]
            send_s[...] = jnp.swapaxes(jnp.stack(cut, axis=0), 0, 1).astype(BF)
            send_all(send_s, got_s, s_send.at[0], s_got.at[0])
            got_s[me] = send_s[me]
            counts = ordered[128:256, :] + ordered[:, 128:256].T + (here_id + 128 == all_id).astype(F32)
            count_b[128:256, :] = counts.astype(BF)
        else:
            wait(in_f.at[pl.ds(0, 127)], h_got.at[it])
            turned = jnp.swapaxes(in_f[...], 0, 1)
            for k in range(4):
                first = jnp.where(core == 0, turned[k], turned[4 + k])
                second = jnp.where(core == 0, turned[4 + k], turned[k])
                for apart in range(2):
                    stack[apart * 128 : apart * 128 + 64, k * 128 : k * 128 + 128] = first[
                        apart * 64 : apart * 64 + 64
                    ]
                    stack[apart * 128 + 64 : apart * 128 + 128, k * 128 : k * 128 + 128] = second[
                        apart * 64 : apart * 64 + 64
                    ]
            total = dot(count_b[...], stack[:, 0:512])
            for apart in range(2):
                part = total[apart * 128 : apart * 128 + 128]
                top = jnp.where(core == 0, part[0:64], part[64:128])
                low = jnp.where(core == 0, part[64:128], part[0:64])
                cut = [v[:, k * 128 : k * 128 + 128] for v in (top, low) for k in range(4)]
                out_f[apart * 64 : apart * 64 + 64] = jnp.swapaxes(jnp.stack(cut, axis=0), 0, 1).astype(BF)
            send_each(
                lambda slot, pcore, apart: out_f.at[apart * 64 + slot],
                lambda apart: got_f.at[me * 2 + core],
                s_send.at[it], s_got.at[it], lead=True,
            )
            got_f[me * 2 + core] = out_f[me]
        wait(sums_got.at[it, pl.ds(0, 15)], sum_rsem.at[it])
        sums = jnp.sum(sums_got[it], axis=0)
        own_sums = jnp.where(core == 0, sums[4:5, :], sums[5:6, :])
        other_sums = jnp.where(core == 0, sums[5:6, :], sums[4:5, :])
        partner = jnp.concatenate([own_sums, other_sums], axis=1)
        spread = [
            jnp.sum(count_f[pl.ds(t * 64 + chip_lane, 1), :] * partner, axis=1, keepdims=True)
            for t in range(tiles)
        ]

        if it == 0:
            wait(got_s.at[pl.ds(0, 63)], s_got.at[it])
        else:
            wait(got_f.at[pl.ds(0, 127)], s_got.at[it])
        news = []
        for t in range(tiles):
            halves = []
            for half in range(2):
                if it == 0:
                    block = got_s[half * 32 : half * 32 + 32].astype(F32)[:, t * 8 : t * 8 + 8, :]
                else:
                    pair = got_f[half * 64 : half * 64 + 64].astype(F32).reshape(32, 2, 8, 128)
                    block = jnp.where(upper, pair[:, t], pair[:, 1 - t])
                    if t:
                        block = pltpu.roll(block, 4, 1)
                halves.append(block.reshape(256, 128))
            mat = jnp.concatenate(halves, axis=1).astype(BF)
            form_sum = jnp.sum(
                esum[t] * dot(mat, cos_b[t]) - ediff[t] * dot(mat, sin_b[t]), axis=0, keepdims=True
            )
            value = (form_sum + spread[t] * (power[t : t + 1] - float(mics))) / scale
            old = estimate[t : t + 1]
            news.append(jnp.maximum(old + (dirty[t : t + 1, :] - value) / diag[t : t + 1], 0.0))
        estimate = jnp.concatenate(news, axis=0)
        if it + 1 < ITERS:
            record = sums_record(estimate)
            rec_send[it + 1] = record
            rec_got[it + 1, row] = record
            cut_by_core(form(estimate))

    out_ref[...] = estimate
    wait(send_h.at[pl.ds(0, 63)], h_send.at[0])
    wait(other_h, x_send)
    wait(send_s.at[pl.ds(0, 63)], s_send.at[0])
    wait(in_f.at[pl.ds(0, 127)], h_send.at[1])
    wait(out_f.at[pl.ds(0, 127)], s_send.at[1])
    for it in range(ITERS):
        wait(rec_got.at[it, pl.ds(0, 7)], rec_ssem.at[it])
        wait(sums_got.at[it, pl.ds(0, 15)], sum_ssem.at[it])
    wait(count_got.at[pl.ds(0, 240)], cnt_ssem)
    wait(part_got.at[pl.ds(0, 7)], part_ssem)


def on_device(phase, dirty_map, pairs, live):
    tiles, mics, width = phase.shape
    vmem, dma = pltpu.VMEM, pltpu.SemaphoreType.DMA
    blocks, fine = vmem((64, 16, 128), BF), vmem((128, 8, 128), BF)
    return pl.pallas_call(
        kernel,
        out_shape=jax.ShapeDtypeStruct(dirty_map.shape, F32),
        in_specs=[pl.BlockSpec(memory_space=pl.ANY)] * 4,
        out_specs=pl.BlockSpec(memory_space=pltpu.VMEM),
        scratch_shapes=[
            vmem((tiles, mics, width), F32),
            vmem((tiles, width), F32),
            vmem((2, pairs.shape[0]), jnp.int32),
            pltpu.SMEM((1,), jnp.int32),
            vmem((tiles, mics, width), BF),
            vmem((tiles, mics, width), BF),
            vmem((tiles, 2 * width, mics), BF),
            vmem((tiles, mics, width), F32),
            vmem((tiles, mics, width), F32),
            blocks, blocks, blocks, blocks, blocks,
            vmem((64, 2, 8, 128), BF), fine, fine, fine,
            vmem((256, 1024), BF),
            vmem((ITERS, 8, 128), F32),
            vmem((ITERS, 8, 8, 128), F32),
            vmem((ITERS, 8, 128), F32),
            vmem((ITERS, 16, 8, 128), F32),
            vmem((16, 128), BF),
            vmem((8, 16, 128), BF),
            vmem((16, 256), BF),
            vmem((256, 256), BF),
            vmem((128, 256), F32),
            vmem((256, 256), BF),
            vmem((256, 256), BF),
            dma((5,)),
            dma((ITERS,)), dma((ITERS,)), dma, dma, dma((ITERS,)), dma((ITERS,)),
            dma((ITERS,)), dma((ITERS,)), dma((ITERS,)), dma((ITERS,)),
            dma, dma, dma, dma,
        ],
        compiler_params=pltpu.CompilerParams(
            collective_id=0, has_side_effects=True, vmem_limit_bytes=48 << 20
        ),
    )(*[pltpu.with_memory_space_constraint(v, pltpu.HBM) for v in (phase, dirty_map, pairs.T)], live)


def solution(mesh):
    in_specs = (
        P(("row", "col"), None, None),
        P(("row", "col"), None),
        P(("row", "col"), None),
        P(("row", "col")),
    )
    out_specs = P(("row", "col"), None)
    return jax.shard_map(
        on_device, mesh=mesh, in_specs=in_specs, out_specs=out_specs, check_vma=False
    )
```

```python
import functools

import jax
import jax.numpy as jnp
from jax import lax
from jax.experimental import pallas as pl
from jax.experimental.pallas import tpu as pltpu
from jax.sharding import PartitionSpec as P

ITERS = 2
LEAD = (1, 0)
MESH = pl.DeviceIdType.MESH
BF = jnp.bfloat16
F32 = jnp.float32
HALF_COS = (0.9999999403953552, -0.1249997615814209, 0.002603973960503936, -2.1646421373588964e-05,
            9.044592985674171e-08)
HALF_SIN = (0.5, -0.020833322778344154, 0.0002604078617878258, -1.5475848158530425e-06,
            5.0883919300304115e-09)


def hops(offset):
    return sum(min(step, 4 - step) for step in offset)


OFFSETS = sorted(
    [(a, b, c) for a in range(4) for b in range(4) for c in range(4) if (a, b, c) != (0, 0, 0)],
    key=lambda offset: (-hops(offset), offset.count(2)),
)
OFFSETS = list(
    dict.fromkeys(o for offset in OFFSETS for o in (offset, tuple(-step % 4 for step in offset)))
)


def polynomial(square, coefficients):
    total = jnp.full_like(square, coefficients[-1])
    for coefficient in coefficients[-2::-1]:
        total = total * square + coefficient
    return total


def dot(a, b):
    return jnp.dot(a, b, preferred_element_type=F32)


def dot_nt(a, b):
    return lax.dot_general(a, b, (((1,), (1,)), ((), ())), preferred_element_type=F32)


def kernel(
    phase_hbm, dirty_hbm, pairs_hbm, live_hbm, out_ref,
    phase, dirty, pairs, live, cos_b, sin_b, points, esum, ediff,
    send_h, own_h, other_h, send_s, got_s, send_f, in_f, out_f, got_f, stack,
    rec_send, rec_got, sums_send, sums_got, part_send, part_got, count_send, count_got, count_f, count_b,
    eye_perm,
    load_sem, h_send, h_got, x_send, x_got, s_send, s_got, rec_ssem, rec_rsem, sum_ssem, sum_rsem,
    part_ssem, part_rsem, cnt_ssem, cnt_rsem,
):
    tiles, mics, width = phase.shape
    scale = float(mics * mics - mics)
    row, col = lax.axis_index("row"), lax.axis_index("col")
    x, core = lax.div(row, 2), lax.rem(row, 2)
    y, z = lax.div(col, 4), lax.rem(col, 4)
    me = col * 4 + x
    other = row + 1 - 2 * core

    barrier = pltpu.get_barrier_semaphore()

    def greet(px, pc, pcore):
        pl.semaphore_signal(
            barrier, inc=1, device_id=(px * 2 + pcore, pc), device_id_type=MESH
        )

    for offset in OFFSETS[:22]:
        px, pc = lax.rem(x + offset[0], 4), lax.rem(y + offset[1], 4) * 4 + lax.rem(z + offset[2], 4)
        greet(px, pc, core)

    loads = [
        pltpu.make_async_copy(phase_hbm.at[0], phase.at[0], load_sem.at[0]),
        pltpu.make_async_copy(phase_hbm.at[1], phase.at[1], load_sem.at[1]),
        pltpu.make_async_copy(dirty_hbm, dirty, load_sem.at[2]),
        pltpu.make_async_copy(pairs_hbm, pairs, load_sem.at[3]),
        pltpu.make_async_copy(live_hbm, live, load_sem.at[4]),
    ]
    for load in loads:
        load.start()

    for offset in OFFSETS[22:]:
        px, pc = lax.rem(x + offset[0], 4), lax.rem(y + offset[1], 4) * 4 + lax.rem(z + offset[2], 4)
        greet(px, pc, core)
    for da in range(4):
        greet(lax.rem(x + da, 4), col, 1 - core)

    lane = lax.broadcasted_iota(jnp.int32, (8, 128), 1)
    sub = lax.broadcasted_iota(jnp.int32, (8, 128), 0)
    chip_lane = col * 4 + x

    def sums_record(estimate):
        record = jnp.zeros((8, 128), F32)
        for t in range(tiles):
            total = jnp.sum(estimate[t : t + 1, :], axis=1, keepdims=True)
            record = jnp.where((sub == 4 + core) & (lane == t * 64 + chip_lane), total, record)
        return record

    def form(estimate):
        mats = []
        row_id = lax.broadcasted_iota(jnp.int32, (mics, mics), 0)
        col_id = lax.broadcasted_iota(jnp.int32, (mics, mics), 1)
        for t in range(tiles):
            value = estimate[t : t + 1, :]
            total = jnp.sum(value, axis=1, keepdims=True)
            left = jnp.concatenate(
                [(esum[t] * value).astype(BF), (ediff[t] * -value).astype(BF)], axis=1
            )
            mat = dot(left, points[t])
            mats.append(jnp.where(row_id == col_id, mat - total, mat))
        return mats

    upper = lax.broadcasted_iota(jnp.int32, (32, 8, 128), 1) < 4

    def cut_by_chip(mats):
        for half in range(2):
            parts = [m[:, half * 128 : half * 128 + 128].reshape(32, 8, 128) for m in mats]
            send_h[pl.ds(half * 32, 32)] = jnp.concatenate(parts, axis=1).astype(BF)

    def cut_by_core(mats):
        for half in range(2):
            first, second = [m[:, half * 128 : half * 128 + 128].reshape(32, 8, 128) for m in mats]
            second = pltpu.roll(second, 4, 1)
            send_f[pl.ds(half * 32, 32), 0] = jnp.where(upper, first, second).astype(BF)
            send_f[pl.ds(half * 32, 32), 1] = jnp.where(upper, second, first).astype(BF)

    def send_each(src, dst, ssem, rsem, lead=False):
        targets = []
        for da, db, dc in OFFSETS + [(0, 0, 0)]:
            px = lax.rem(x + da, 4)
            pc = lax.rem(y + db, 4) * 4 + lax.rem(z + dc, 4)
            for apart in range(2):
                if (da, db, dc) != (0, 0, 0) or apart:
                    targets.append((px * 2 + (1 - core if apart else core), pc))
        for place, ahead in enumerate(LEAD if lead else ()):
            first_row, first_col = targets[place]
            mine = (row == ahead) & (col == 0)
            moved = [(jnp.where(mine, first_row, ahead), jnp.where(mine, first_col, 0))]
            for prow, pcol in targets[place + 1 :]:
                hit = (prow == ahead) & (pcol == 0)
                moved.append((jnp.where(hit, first_row, prow), jnp.where(hit, first_col, pcol)))
            targets = targets[:place] + moved
        for prow, pcol in targets:
            slot, pcore = pcol * 4 + lax.div(prow, 2), lax.rem(prow, 2)
            apart = lax.rem(core + pcore, 2)
            pltpu.make_async_remote_copy(
                src_ref=src(slot, pcore, apart), dst_ref=dst(apart), send_sem=ssem, recv_sem=rsem,
                device_id=(prow, pcol), device_id_type=MESH,
            ).start()

    def send_all(src, dst, ssem, rsem):
        for da, db, dc in OFFSETS:
            px = lax.rem(x + da, 4)
            pc = lax.rem(y + db, 4) * 4 + lax.rem(z + dc, 4)
            pltpu.make_async_remote_copy(
                src_ref=src.at[pc * 4 + px], dst_ref=dst.at[me], send_sem=ssem, recv_sem=rsem,
                device_id=(px * 2 + core, pc), device_id_type=MESH,
            ).start()

    def send_row(src, dst, ssem, rsem):
        for k in (4, 5, 3, 2, 6, 7, 1):
            pltpu.make_async_remote_copy(
                src_ref=src, dst_ref=dst.at[row], send_sem=ssem, recv_sem=rsem,
                device_id=(lax.rem(row + k, 8), col), device_id_type=MESH,
            ).start()

    def send_col(src, dst, ssem, rsem):
        for da, db, dc in OFFSETS:
            if da == 0:
                pltpu.make_async_remote_copy(
                    src_ref=src, dst_ref=dst, send_sem=ssem, recv_sem=rsem,
                    device_id=(row, lax.rem(y + db, 4) * 4 + lax.rem(z + dc, 4)), device_id_type=MESH,
                ).start()

    def wait(ref, sem):
        pltpu.make_async_copy(ref, ref, sem).wait()

    loads[2].wait()
    powers, diags, firsts = [], [], []
    for t in range(tiles):
        loads[t].wait()
        angle = phase[t]
        square = angle * angle
        half_sine = polynomial(square, HALF_SIN) * angle
        twice = half_sine + half_sine
        cosine = (1.0 - twice * half_sine).astype(BF)
        sine = (twice * polynomial(square, HALF_COS)).astype(BF)
        cos_b[t] = cosine
        sin_b[t] = sine
        cosine, sine = cosine.astype(F32), sine.astype(F32)
        esum[t] = cosine + sine
        ediff[t] = cosine - sine
        power = jnp.sum(cosine * cosine + sine * sine, axis=0, keepdims=True)
        diag = (power * power - float(mics)) / scale
        powers.append(power)
        diags.append(diag)
        firsts.append(jnp.maximum(dirty[t : t + 1, :] / diag, 0.0))
        points[t] = jnp.concatenate([cosine.T, sine.T], axis=0).astype(BF)
    power = jnp.concatenate(powers, axis=0)
    diag = jnp.concatenate(diags, axis=0)
    estimate = jnp.concatenate(firsts, axis=0)

    loads[3].wait()
    loads[4].wait()
    slots = pairs.shape[1]
    first, second = pairs[0:1, :], pairs[1:2, :]
    first_lane = (first & 1) * 64 + ((first >> 1) & 15) * 4 + (first >> 6)
    second_row = (second >> 5) * 2 + (second & 1)
    listed = lax.broadcasted_iota(jnp.int32, (128, slots), 1) < live[0]
    first_hot = (lax.broadcasted_iota(jnp.int32, (128, slots), 0) == first_lane) & listed
    second_hot = lax.broadcasted_iota(jnp.int32, (16, slots), 0) == second_row
    part_send[...] = dot_nt(
        second_hot.astype(F32).astype(BF), first_hot.astype(F32).astype(BF)
    ).astype(BF)
    part_got[row] = part_send[...]
    record = sums_record(estimate)
    rec_send[0] = record
    rec_got[0, row] = record
    cut_by_chip(form(estimate))

    raw = lax.broadcasted_iota(jnp.int32, (256, 256), 1)
    raw_row = (raw >> 1) & 7
    placed = (((raw_row + core) & 1) << 7) + ((raw & 1) << 6) + ((raw >> 4) << 2) + (raw_row >> 1)
    eye_perm[...] = (lax.broadcasted_iota(jnp.int32, (256, 256), 0) == placed).astype(F32).astype(BF)

    pl.semaphore_wait(barrier, len(OFFSETS) + 4)

    for it in range(ITERS):
        if it == 0:
            send_row(part_send, part_got, part_ssem, part_rsem)
            send_all(send_h, own_h, h_send.at[0], h_got.at[0])
            own_h[me] = send_h[me]
            wait(part_got.at[pl.ds(0, 7)], part_rsem)
            by_core = [
                sum(part_got[2 * k + c].astype(F32) for k in range(4)).astype(BF) for c in range(2)
            ]
            count_send[:, 0:128] = jnp.where(core == 0, by_core[0], by_core[1])
            count_send[:, 128:256] = jnp.where(core == 0, by_core[1], by_core[0])
            here = pl.ds(pl.multiple_of(col * 16, 16), 16)
            count_got[here, :] = count_send[...]
            send_col(count_send, count_got.at[here], cnt_ssem, cnt_rsem)
            send_row(rec_send.at[0], rec_got.at[0], rec_ssem.at[0], rec_rsem.at[0])
            wait(own_h.at[pl.ds(0, 63)], h_got.at[0])
            exchange = pltpu.make_async_remote_copy(
                src_ref=own_h, dst_ref=other_h, send_sem=x_send, recv_sem=x_got,
                device_id=(other, col), device_id_type=MESH,
            )
            exchange.start()
        else:
            send_each(
                lambda slot, pcore, apart: send_f.at[slot, pcore],
                lambda apart: in_f.at[apart * 64 + me],
                h_send.at[it], h_got.at[it],
            )
            record = sums_record(estimate)
            rec_send[it] = record
            rec_got[it, row] = record
            send_row(rec_send.at[it], rec_got.at[it], rec_ssem.at[it], rec_rsem.at[it])
            in_f[me] = send_f[me, core]

        wait(rec_got.at[it, pl.ds(0, 7)], rec_rsem.at[it])
        record = jnp.sum(rec_got[it], axis=0)
        sums_send[it] = record
        sums_got[it, col] = record
        send_col(sums_send.at[it], sums_got.at[it, col], sum_ssem.at[it], sum_rsem.at[it])

        if it == 0:
            for base, source in ((0, own_h), (128, other_h)):
                if base:
                    exchange.wait_recv()
                turned = jnp.swapaxes(source[...], 0, 1)
                for k in range(16):
                    stack[base + (k // 8) * 64 : base + (k // 8) * 64 + 64,
                          (k % 8) * 128 : (k % 8) * 128 + 128] = turned[k]
            wait(count_got.at[pl.ds(0, 240)], cnt_rsem)
            ordered = dot(eye_perm[...], count_got[...])
            here_id = lax.broadcasted_iota(jnp.int32, (128, 256), 0)
            all_id = lax.broadcasted_iota(jnp.int32, (128, 256), 1)
            counts = ordered[0:128, :] + ordered[:, 0:128].T + (here_id == all_id).astype(F32)
            count_f[...] = counts
            count_b[0:128, :] = counts.astype(BF)
            total = dot(count_b[0:128, :], stack[...])
            cut = [
                total[(k // 8) * 64 : (k // 8) * 64 + 64, (k % 8) * 128 : (k % 8) * 128 + 128]
                for k in range(16)
            ]
            send_s[...] = jnp.swapaxes(jnp.stack(cut, axis=0), 0, 1).astype(BF)
            send_all(send_s, got_s, s_send.at[0], s_got.at[0])
            got_s[me] = send_s[me]
            counts = ordered[128:256, :] + ordered[:, 128:256].T + (here_id + 128 == all_id).astype(F32)
            count_b[128:256, :] = counts.astype(BF)
        else:
            wait(in_f.at[pl.ds(0, 127)], h_got.at[it])
            turned = jnp.swapaxes(in_f[...], 0, 1)
            for k in range(4):
                first = jnp.where(core == 0, turned[k], turned[4 + k])
                second = jnp.where(core == 0, turned[4 + k], turned[k])
                for apart in range(2):
                    stack[apart * 128 : apart * 128 + 64, k * 128 : k * 128 + 128] = first[
                        apart * 64 : apart * 64 + 64
                    ]
                    stack[apart * 128 + 64 : apart * 128 + 128, k * 128 : k * 128 + 128] = second[
                        apart * 64 : apart * 64 + 64
                    ]
            total = dot(count_b[...], stack[:, 0:512])
            for apart in range(2):
                part = total[apart * 128 : apart * 128 + 128]
                top = jnp.where(core == 0, part[0:64], part[64:128])
                low = jnp.where(core == 0, part[64:128], part[0:64])
                cut = [v[:, k * 128 : k * 128 + 128] for v in (top, low) for k in range(4)]
                out_f[apart * 64 : apart * 64 + 64] = jnp.swapaxes(jnp.stack(cut, axis=0), 0, 1).astype(BF)
            send_each(
                lambda slot, pcore, apart: out_f.at[apart * 64 + slot],
                lambda apart: got_f.at[me * 2 + core],
                s_send.at[it], s_got.at[it], lead=True,
            )
            got_f[me * 2 + core] = out_f[me]
        wait(sums_got.at[it, pl.ds(0, 15)], sum_rsem.at[it])
        sums = jnp.sum(sums_got[it], axis=0)
        own_sums = jnp.where(core == 0, sums[4:5, :], sums[5:6, :])
        other_sums = jnp.where(core == 0, sums[5:6, :], sums[4:5, :])
        partner = jnp.concatenate([own_sums, other_sums], axis=1)
        spread = [
            jnp.sum(count_f[pl.ds(t * 64 + chip_lane, 1), :] * partner, axis=1, keepdims=True)
            for t in range(tiles)
        ]

        if it == 0:
            wait(got_s.at[pl.ds(0, 63)], s_got.at[it])
        else:
            wait(got_f.at[pl.ds(0, 127)], s_got.at[it])
        news = []
        for t in range(tiles):
            halves = []
            for half in range(2):
                if it == 0:
                    block = got_s[half * 32 : half * 32 + 32].astype(F32)[:, t * 8 : t * 8 + 8, :]
                else:
                    pair = got_f[half * 64 : half * 64 + 64].astype(F32).reshape(32, 2, 8, 128)
                    block = jnp.where(upper, pair[:, t], pair[:, 1 - t])
                    if t:
                        block = pltpu.roll(block, 4, 1)
                halves.append(block.reshape(256, 128))
            mat = jnp.concatenate(halves, axis=1).astype(BF)
            form_sum = jnp.sum(
                esum[t] * dot(mat, cos_b[t]) - ediff[t] * dot(mat, sin_b[t]), axis=0, keepdims=True
            )
            value = (form_sum + spread[t] * (power[t : t + 1] - float(mics))) / scale
            old = estimate[t : t + 1]
            news.append(jnp.maximum(old + (dirty[t : t + 1, :] - value) / diag[t : t + 1], 0.0))
        estimate = jnp.concatenate(news, axis=0)
        if it + 1 < ITERS:
            cut_by_core(form(estimate))

    out_ref[...] = estimate
    wait(send_h.at[pl.ds(0, 63)], h_send.at[0])
    wait(other_h, x_send)
    wait(send_s.at[pl.ds(0, 63)], s_send.at[0])
    wait(in_f.at[pl.ds(0, 127)], h_send.at[1])
    wait(out_f.at[pl.ds(0, 127)], s_send.at[1])
    for it in range(ITERS):
        wait(rec_got.at[it, pl.ds(0, 7)], rec_ssem.at[it])
        wait(sums_got.at[it, pl.ds(0, 15)], sum_ssem.at[it])
    wait(count_got.at[pl.ds(0, 240)], cnt_ssem)
    wait(part_got.at[pl.ds(0, 7)], part_ssem)


def on_device(phase, dirty_map, pairs, live):
    tiles, mics, width = phase.shape
    vmem, dma = pltpu.VMEM, pltpu.SemaphoreType.DMA
    blocks, fine = vmem((64, 16, 128), BF), vmem((128, 8, 128), BF)
    return pl.pallas_call(
        kernel,
        out_shape=jax.ShapeDtypeStruct(dirty_map.shape, F32),
        in_specs=[pl.BlockSpec(memory_space=pl.ANY)] * 4,
        out_specs=pl.BlockSpec(memory_space=pltpu.VMEM),
        scratch_shapes=[
            vmem((tiles, mics, width), F32),
            vmem((tiles, width), F32),
            vmem((2, pairs.shape[0]), jnp.int32),
            pltpu.SMEM((1,), jnp.int32),
            vmem((tiles, mics, width), BF),
            vmem((tiles, mics, width), BF),
            vmem((tiles, 2 * width, mics), BF),
            vmem((tiles, mics, width), F32),
            vmem((tiles, mics, width), F32),
            blocks, blocks, blocks, blocks, blocks,
            vmem((64, 2, 8, 128), BF), fine, fine, fine,
            vmem((256, 1024), BF),
            vmem((ITERS, 8, 128), F32),
            vmem((ITERS, 8, 8, 128), F32),
            vmem((ITERS, 8, 128), F32),
            vmem((ITERS, 16, 8, 128), F32),
            vmem((16, 128), BF),
            vmem((8, 16, 128), BF),
            vmem((16, 256), BF),
            vmem((256, 256), BF),
            vmem((128, 256), F32),
            vmem((256, 256), BF),
            vmem((256, 256), BF),
            dma((5,)),
            dma((ITERS,)), dma((ITERS,)), dma, dma, dma((ITERS,)), dma((ITERS,)),
            dma((ITERS,)), dma((ITERS,)), dma((ITERS,)), dma((ITERS,)),
            dma, dma, dma, dma,
        ],
        compiler_params=pltpu.CompilerParams(
            collective_id=0, has_side_effects=True, vmem_limit_bytes=48 << 20
        ),
    )(*[pltpu.with_memory_space_constraint(v, pltpu.HBM) for v in (phase, dirty_map, pairs.T)], live)


def solution(mesh):
    in_specs = (
        P(("row", "col"), None, None),
        P(("row", "col"), None),
        P(("row", "col"), None),
        P(("row", "col")),
    )
    out_specs = P(("row", "col"), None)
    return jax.shard_map(
        on_device, mesh=mesh, in_specs=in_specs, out_specs=out_specs, check_vma=False
    )
```

```python
import functools

import jax
import jax.numpy as jnp
from jax import lax
from jax.experimental import pallas as pl
from jax.experimental.pallas import tpu as pltpu
from jax.sharding import PartitionSpec as P

ITERS = 2
LEAD = (1, 0)
MESH = pl.DeviceIdType.MESH
BF = jnp.bfloat16
F32 = jnp.float32
HALF_COS = (0.9999999403953552, -0.1249997615814209, 0.002603973960503936, -2.1646421373588964e-05,
            9.044592985674171e-08)
HALF_SIN = (0.5, -0.020833322778344154, 0.0002604078617878258, -1.5475848158530425e-06,
            5.0883919300304115e-09)


def hops(offset):
    return sum(min(step, 4 - step) for step in offset)


OFFSETS = sorted(
    [(a, b, c) for a in range(4) for b in range(4) for c in range(4) if (a, b, c) != (0, 0, 0)],
    key=lambda offset: (-hops(offset), offset.count(2)),
)
OFFSETS = list(
    dict.fromkeys(o for offset in OFFSETS for o in (offset, tuple(-step % 4 for step in offset)))
)


def polynomial(square, coefficients):
    total = jnp.full_like(square, coefficients[-1])
    for coefficient in coefficients[-2::-1]:
        total = total * square + coefficient
    return total


def dot(a, b):
    return jnp.dot(a, b, preferred_element_type=F32)


def dot_nt(a, b):
    return lax.dot_general(a, b, (((1,), (1,)), ((), ())), preferred_element_type=F32)


def kernel(
    phase_hbm, dirty_hbm, pairs_hbm, live_hbm, out_ref,
    phase, dirty, pairs, live, cos_b, sin_b, points, esum, ediff,
    send_h, own_h, other_h, send_s, got_s, send_f, in_f, out_f, got_f, stack,
    rec_send, rec_got, sums_send, sums_got, part_send, part_got, count_send, count_got, count_f, count_b,
    eye_perm,
    load_sem, h_send, h_got, x_send, x_got, s_send, s_got, rec_ssem, rec_rsem, sum_ssem, sum_rsem,
    part_ssem, part_rsem, cnt_ssem, cnt_rsem,
):
    tiles, mics, width = phase.shape
    scale = float(mics * mics - mics)
    row, col = lax.axis_index("row"), lax.axis_index("col")
    x, core = lax.div(row, 2), lax.rem(row, 2)
    y, z = lax.div(col, 4), lax.rem(col, 4)
    me = col * 4 + x
    other = row + 1 - 2 * core

    barrier = pltpu.get_barrier_semaphore()

    def greet(px, pc, pcore):
        pl.semaphore_signal(
            barrier, inc=1, device_id=(px * 2 + pcore, pc), device_id_type=MESH
        )

    for offset in OFFSETS[:22]:
        px, pc = lax.rem(x + offset[0], 4), lax.rem(y + offset[1], 4) * 4 + lax.rem(z + offset[2], 4)
        greet(px, pc, core)

    loads = [
        pltpu.make_async_copy(phase_hbm.at[0], phase.at[0], load_sem.at[0]),
        pltpu.make_async_copy(phase_hbm.at[1], phase.at[1], load_sem.at[1]),
        pltpu.make_async_copy(dirty_hbm, dirty, load_sem.at[2]),
        pltpu.make_async_copy(pairs_hbm, pairs, load_sem.at[3]),
        pltpu.make_async_copy(live_hbm, live, load_sem.at[4]),
    ]
    for load in loads:
        load.start()

    for offset in OFFSETS[22:]:
        px, pc = lax.rem(x + offset[0], 4), lax.rem(y + offset[1], 4) * 4 + lax.rem(z + offset[2], 4)
        greet(px, pc, core)
    for da in range(4):
        greet(lax.rem(x + da, 4), col, 1 - core)

    lane = lax.broadcasted_iota(jnp.int32, (8, 128), 1)
    sub = lax.broadcasted_iota(jnp.int32, (8, 128), 0)
    chip_lane = col * 4 + x

    def sums_record(estimate):
        record = jnp.zeros((8, 128), F32)
        for t in range(tiles):
            total = jnp.sum(estimate[t : t + 1, :], axis=1, keepdims=True)
            record = jnp.where((sub == 4 + core) & (lane == t * 64 + chip_lane), total, record)
        return record

    def form(estimate):
        mats = []
        row_id = lax.broadcasted_iota(jnp.int32, (mics, mics), 0)
        col_id = lax.broadcasted_iota(jnp.int32, (mics, mics), 1)
        for t in range(tiles):
            value = estimate[t : t + 1, :]
            total = jnp.sum(value, axis=1, keepdims=True)
            left = jnp.concatenate(
                [(esum[t] * value).astype(BF), (ediff[t] * -value).astype(BF)], axis=1
            )
            mat = dot(left, points[t])
            mats.append(jnp.where(row_id == col_id, mat - total, mat))
        return mats

    upper = lax.broadcasted_iota(jnp.int32, (32, 8, 128), 1) < 4

    def cut_by_chip(mats):
        for half in range(2):
            parts = [m[:, half * 128 : half * 128 + 128].reshape(32, 8, 128) for m in mats]
            send_h[pl.ds(half * 32, 32)] = jnp.concatenate(parts, axis=1).astype(BF)

    def cut_by_core(mats):
        for half in range(2):
            first, second = [m[:, half * 128 : half * 128 + 128].reshape(32, 8, 128) for m in mats]
            second = pltpu.roll(second, 4, 1)
            send_f[pl.ds(half * 32, 32), 0] = jnp.where(upper, first, second).astype(BF)
            send_f[pl.ds(half * 32, 32), 1] = jnp.where(upper, second, first).astype(BF)

    def send_each(src, dst, ssem, rsem, lead=False, midway=None):
        targets = []
        for da, db, dc in OFFSETS + [(0, 0, 0)]:
            px = lax.rem(x + da, 4)
            pc = lax.rem(y + db, 4) * 4 + lax.rem(z + dc, 4)
            for apart in range(2):
                if (da, db, dc) != (0, 0, 0) or apart:
                    targets.append((px * 2 + (1 - core if apart else core), pc))
        for place, ahead in enumerate(LEAD if lead else ()):
            first_row, first_col = targets[place]
            mine = (row == ahead) & (col == 0)
            moved = [(jnp.where(mine, first_row, ahead), jnp.where(mine, first_col, 0))]
            for prow, pcol in targets[place + 1 :]:
                hit = (prow == ahead) & (pcol == 0)
                moved.append((jnp.where(hit, first_row, prow), jnp.where(hit, first_col, pcol)))
            targets = targets[:place] + moved
        for place, (prow, pcol) in enumerate(targets):
            if midway is not None and place == 64:
                midway()
            slot, pcore = pcol * 4 + lax.div(prow, 2), lax.rem(prow, 2)
            apart = lax.rem(core + pcore, 2)
            pltpu.make_async_remote_copy(
                src_ref=src(slot, pcore, apart), dst_ref=dst(apart), send_sem=ssem, recv_sem=rsem,
                device_id=(prow, pcol), device_id_type=MESH,
            ).start()

    def send_all(src, dst, ssem, rsem):
        for da, db, dc in OFFSETS:
            px = lax.rem(x + da, 4)
            pc = lax.rem(y + db, 4) * 4 + lax.rem(z + dc, 4)
            pltpu.make_async_remote_copy(
                src_ref=src.at[pc * 4 + px], dst_ref=dst.at[me], send_sem=ssem, recv_sem=rsem,
                device_id=(px * 2 + core, pc), device_id_type=MESH,
            ).start()

    def send_row(src, dst, ssem, rsem):
        for k in (4, 5, 3, 2, 6, 7, 1):
            pltpu.make_async_remote_copy(
                src_ref=src, dst_ref=dst.at[row], send_sem=ssem, recv_sem=rsem,
                device_id=(lax.rem(row + k, 8), col), device_id_type=MESH,
            ).start()

    def send_col(src, dst, ssem, rsem):
        for da, db, dc in OFFSETS:
            if da == 0:
                pltpu.make_async_remote_copy(
                    src_ref=src, dst_ref=dst, send_sem=ssem, recv_sem=rsem,
                    device_id=(row, lax.rem(y + db, 4) * 4 + lax.rem(z + dc, 4)), device_id_type=MESH,
                ).start()

    def wait(ref, sem):
        pltpu.make_async_copy(ref, ref, sem).wait()

    loads[2].wait()
    powers, diags, firsts = [], [], []
    for t in range(tiles):
        loads[t].wait()
        angle = phase[t]
        square = angle * angle
        half_sine = polynomial(square, HALF_SIN) * angle
        twice = half_sine + half_sine
        cosine = (1.0 - twice * half_sine).astype(BF)
        sine = (twice * polynomial(square, HALF_COS)).astype(BF)
        cos_b[t] = cosine
        sin_b[t] = sine
        cosine, sine = cosine.astype(F32), sine.astype(F32)
        esum[t] = cosine + sine
        ediff[t] = cosine - sine
        power = jnp.sum(cosine * cosine + sine * sine, axis=0, keepdims=True)
        diag = (power * power - float(mics)) / scale
        powers.append(power)
        diags.append(diag)
        firsts.append(jnp.maximum(dirty[t : t + 1, :] / diag, 0.0))
        points[t] = jnp.concatenate([cosine.T, sine.T], axis=0).astype(BF)
    power = jnp.concatenate(powers, axis=0)
    diag = jnp.concatenate(diags, axis=0)
    estimate = jnp.concatenate(firsts, axis=0)

    loads[3].wait()
    loads[4].wait()
    slots = pairs.shape[1]
    first, second = pairs[0:1, :], pairs[1:2, :]
    first_lane = (first & 1) * 64 + ((first >> 1) & 15) * 4 + (first >> 6)
    second_row = (second >> 5) * 2 + (second & 1)
    listed = lax.broadcasted_iota(jnp.int32, (128, slots), 1) < live[0]
    first_hot = (lax.broadcasted_iota(jnp.int32, (128, slots), 0) == first_lane) & listed
    second_hot = lax.broadcasted_iota(jnp.int32, (16, slots), 0) == second_row
    part_send[...] = dot_nt(
        second_hot.astype(F32).astype(BF), first_hot.astype(F32).astype(BF)
    ).astype(BF)
    part_got[row] = part_send[...]
    record = sums_record(estimate)
    rec_send[0] = record
    rec_got[0, row] = record
    cut_by_chip(form(estimate))

    raw = lax.broadcasted_iota(jnp.int32, (256, 256), 1)
    raw_row = (raw >> 1) & 7
    placed = (((raw_row + core) & 1) << 7) + ((raw & 1) << 6) + ((raw >> 4) << 2) + (raw_row >> 1)
    eye_perm[...] = (lax.broadcasted_iota(jnp.int32, (256, 256), 0) == placed).astype(F32).astype(BF)

    pl.semaphore_wait(barrier, len(OFFSETS) + 4)

    for it in range(ITERS):
        if it == 0:
            send_row(part_send, part_got, part_ssem, part_rsem)
            send_all(send_h, own_h, h_send.at[0], h_got.at[0])
            own_h[me] = send_h[me]
            wait(part_got.at[pl.ds(0, 7)], part_rsem)
            by_core = [
                sum(part_got[2 * k + c].astype(F32) for k in range(4)).astype(BF) for c in range(2)
            ]
            count_send[:, 0:128] = jnp.where(core == 0, by_core[0], by_core[1])
            count_send[:, 128:256] = jnp.where(core == 0, by_core[1], by_core[0])
            here = pl.ds(pl.multiple_of(col * 16, 16), 16)
            count_got[here, :] = count_send[...]
            send_col(count_send, count_got.at[here], cnt_ssem, cnt_rsem)
            send_row(rec_send.at[0], rec_got.at[0], rec_ssem.at[0], rec_rsem.at[0])
            wait(own_h.at[pl.ds(0, 63)], h_got.at[0])
            exchange = pltpu.make_async_remote_copy(
                src_ref=own_h, dst_ref=other_h, send_sem=x_send, recv_sem=x_got,
                device_id=(other, col), device_id_type=MESH,
            )
            exchange.start()
        else:
            def send_sums():
                record = sums_record(estimate)
                rec_send[it] = record
                rec_got[it, row] = record
                send_row(rec_send.at[it], rec_got.at[it], rec_ssem.at[it], rec_rsem.at[it])

            send_each(
                lambda slot, pcore, apart: send_f.at[slot, pcore],
                lambda apart: in_f.at[apart * 64 + me],
                h_send.at[it], h_got.at[it], midway=send_sums,
            )
            in_f[me] = send_f[me, core]

        wait(rec_got.at[it, pl.ds(0, 7)], rec_rsem.at[it])
        record = jnp.sum(rec_got[it], axis=0)
        sums_send[it] = record
        sums_got[it, col] = record
        send_col(sums_send.at[it], sums_got.at[it, col], sum_ssem.at[it], sum_rsem.at[it])

        if it == 0:
            for base, source in ((0, own_h), (128, other_h)):
                if base:
                    exchange.wait_recv()
                turned = jnp.swapaxes(source[...], 0, 1)
                for k in range(16):
                    stack[base + (k // 8) * 64 : base + (k // 8) * 64 + 64,
                          (k % 8) * 128 : (k % 8) * 128 + 128] = turned[k]
            wait(count_got.at[pl.ds(0, 240)], cnt_rsem)
            ordered = dot(eye_perm[...], count_got[...])
            here_id = lax.broadcasted_iota(jnp.int32, (128, 256), 0)
            all_id = lax.broadcasted_iota(jnp.int32, (128, 256), 1)
            counts = ordered[0:128, :] + ordered[:, 0:128].T + (here_id == all_id).astype(F32)
            count_f[...] = counts
            count_b[0:128, :] = counts.astype(BF)
            total = dot(count_b[0:128, :], stack[...])
            cut = [
                total[(k // 8) * 64 : (k // 8) * 64 + 64, (k % 8) * 128 : (k % 8) * 128 + 128]
                for k in range(16)
            ]
            send_s[...] = jnp.swapaxes(jnp.stack(cut, axis=0), 0, 1).astype(BF)
            send_all(send_s, got_s, s_send.at[0], s_got.at[0])
            got_s[me] = send_s[me]
            counts = ordered[128:256, :] + ordered[:, 128:256].T + (here_id + 128 == all_id).astype(F32)
            count_b[128:256, :] = counts.astype(BF)
        else:
            wait(in_f.at[pl.ds(0, 127)], h_got.at[it])
            turned = jnp.swapaxes(in_f[...], 0, 1)
            for k in range(4):
                first = jnp.where(core == 0, turned[k], turned[4 + k])
                second = jnp.where(core == 0, turned[4 + k], turned[k])
                for apart in range(2):
                    stack[apart * 128 : apart * 128 + 64, k * 128 : k * 128 + 128] = first[
                        apart * 64 : apart * 64 + 64
                    ]
                    stack[apart * 128 + 64 : apart * 128 + 128, k * 128 : k * 128 + 128] = second[
                        apart * 64 : apart * 64 + 64
                    ]
            total = dot(count_b[...], stack[:, 0:512])
            for apart in range(2):
                part = total[apart * 128 : apart * 128 + 128]
                top = jnp.where(core == 0, part[0:64], part[64:128])
                low = jnp.where(core == 0, part[64:128], part[0:64])
                cut = [v[:, k * 128 : k * 128 + 128] for v in (top, low) for k in range(4)]
                out_f[apart * 64 : apart * 64 + 64] = jnp.swapaxes(jnp.stack(cut, axis=0), 0, 1).astype(BF)
            send_each(
                lambda slot, pcore, apart: out_f.at[apart * 64 + slot],
                lambda apart: got_f.at[me * 2 + core],
                s_send.at[it], s_got.at[it], lead=True,
            )
            got_f[me * 2 + core] = out_f[me]
        wait(sums_got.at[it, pl.ds(0, 15)], sum_rsem.at[it])
        sums = jnp.sum(sums_got[it], axis=0)
        own_sums = jnp.where(core == 0, sums[4:5, :], sums[5:6, :])
        other_sums = jnp.where(core == 0, sums[5:6, :], sums[4:5, :])
        partner = jnp.concatenate([own_sums, other_sums], axis=1)
        spread = [
            jnp.sum(count_f[pl.ds(t * 64 + chip_lane, 1), :] * partner, axis=1, keepdims=True)
            for t in range(tiles)
        ]

        if it == 0:
            wait(got_s.at[pl.ds(0, 63)], s_got.at[it])
        else:
            wait(got_f.at[pl.ds(0, 127)], s_got.at[it])
        news = []
        for t in range(tiles):
            halves = []
            for half in range(2):
                if it == 0:
                    block = got_s[half * 32 : half * 32 + 32].astype(F32)[:, t * 8 : t * 8 + 8, :]
                else:
                    pair = got_f[half * 64 : half * 64 + 64].astype(F32).reshape(32, 2, 8, 128)
                    block = jnp.where(upper, pair[:, t], pair[:, 1 - t])
                    if t:
                        block = pltpu.roll(block, 4, 1)
                halves.append(block.reshape(256, 128))
            mat = jnp.concatenate(halves, axis=1).astype(BF)
            form_sum = jnp.sum(
                esum[t] * dot(mat, cos_b[t]) - ediff[t] * dot(mat, sin_b[t]), axis=0, keepdims=True
            )
            value = (form_sum + spread[t] * (power[t : t + 1] - float(mics))) / scale
            old = estimate[t : t + 1]
            news.append(jnp.maximum(old + (dirty[t : t + 1, :] - value) / diag[t : t + 1], 0.0))
        estimate = jnp.concatenate(news, axis=0)
        if it + 1 < ITERS:
            cut_by_core(form(estimate))

    out_ref[...] = estimate
    wait(send_h.at[pl.ds(0, 63)], h_send.at[0])
    wait(other_h, x_send)
    wait(send_s.at[pl.ds(0, 63)], s_send.at[0])
    wait(in_f.at[pl.ds(0, 127)], h_send.at[1])
    wait(out_f.at[pl.ds(0, 127)], s_send.at[1])
    for it in range(ITERS):
        wait(rec_got.at[it, pl.ds(0, 7)], rec_ssem.at[it])
        wait(sums_got.at[it, pl.ds(0, 15)], sum_ssem.at[it])
    wait(count_got.at[pl.ds(0, 240)], cnt_ssem)
    wait(part_got.at[pl.ds(0, 7)], part_ssem)


def on_device(phase, dirty_map, pairs, live):
    tiles, mics, width = phase.shape
    vmem, dma = pltpu.VMEM, pltpu.SemaphoreType.DMA
    blocks, fine = vmem((64, 16, 128), BF), vmem((128, 8, 128), BF)
    return pl.pallas_call(
        kernel,
        out_shape=jax.ShapeDtypeStruct(dirty_map.shape, F32),
        in_specs=[pl.BlockSpec(memory_space=pl.ANY)] * 4,
        out_specs=pl.BlockSpec(memory_space=pltpu.VMEM),
        scratch_shapes=[
            vmem((tiles, mics, width), F32),
            vmem((tiles, width), F32),
            vmem((2, pairs.shape[0]), jnp.int32),
            pltpu.SMEM((1,), jnp.int32),
            vmem((tiles, mics, width), BF),
            vmem((tiles, mics, width), BF),
            vmem((tiles, 2 * width, mics), BF),
            vmem((tiles, mics, width), F32),
            vmem((tiles, mics, width), F32),
            blocks, blocks, blocks, blocks, blocks,
            vmem((64, 2, 8, 128), BF), fine, fine, fine,
            vmem((256, 1024), BF),
            vmem((ITERS, 8, 128), F32),
            vmem((ITERS, 8, 8, 128), F32),
            vmem((ITERS, 8, 128), F32),
            vmem((ITERS, 16, 8, 128), F32),
            vmem((16, 128), BF),
            vmem((8, 16, 128), BF),
            vmem((16, 256), BF),
            vmem((256, 256), BF),
            vmem((128, 256), F32),
            vmem((256, 256), BF),
            vmem((256, 256), BF),
            dma((5,)),
            dma((ITERS,)), dma((ITERS,)), dma, dma, dma((ITERS,)), dma((ITERS,)),
            dma((ITERS,)), dma((ITERS,)), dma((ITERS,)), dma((ITERS,)),
            dma, dma, dma, dma,
        ],
        compiler_params=pltpu.CompilerParams(
            collective_id=0, has_side_effects=True, vmem_limit_bytes=48 << 20
        ),
    )(*[pltpu.with_memory_space_constraint(v, pltpu.HBM) for v in (phase, dirty_map, pairs.T)], live)


def solution(mesh):
    in_specs = (
        P(("row", "col"), None, None),
        P(("row", "col"), None),
        P(("row", "col"), None),
        P(("row", "col")),
    )
    out_specs = P(("row", "col"), None)
    return jax.shard_map(
        on_device, mesh=mesh, in_specs=in_specs, out_specs=out_specs, check_vma=False
    )
```

```python
import functools

import jax
import jax.numpy as jnp
from jax import lax
from jax.experimental import pallas as pl
from jax.experimental.pallas import tpu as pltpu
from jax.sharding import PartitionSpec as P

ITERS = 2
LEAD = (1, 0)
MESH = pl.DeviceIdType.MESH
BF = jnp.bfloat16
F32 = jnp.float32
HALF_COS = (0.9999999403953552, -0.1249997615814209, 0.002603973960503936, -2.1646421373588964e-05,
            9.044592985674171e-08)
HALF_SIN = (0.5, -0.020833322778344154, 0.0002604078617878258, -1.5475848158530425e-06,
            5.0883919300304115e-09)


def hops(offset):
    return sum(min(step, 4 - step) for step in offset)


OFFSETS = sorted(
    [(a, b, c) for a in range(4) for b in range(4) for c in range(4) if (a, b, c) != (0, 0, 0)],
    key=lambda offset: (-hops(offset), offset.count(2), offset[0] == 2),
)
OFFSETS = list(
    dict.fromkeys(o for offset in OFFSETS for o in (offset, tuple(-step % 4 for step in offset)))
)


def polynomial(square, coefficients):
    total = jnp.full_like(square, coefficients[-1])
    for coefficient in coefficients[-2::-1]:
        total = total * square + coefficient
    return total


def dot(a, b):
    return jnp.dot(a, b, preferred_element_type=F32)


def dot_nt(a, b):
    return lax.dot_general(a, b, (((1,), (1,)), ((), ())), preferred_element_type=F32)


def kernel(
    phase_hbm, dirty_hbm, pairs_hbm, live_hbm, out_ref,
    phase, dirty, pairs, live, cos_b, sin_b, points, esum, ediff,
    send_h, own_h, other_h, send_s, got_s, send_f, in_f, out_f, got_f, stack,
    rec_send, rec_got, sums_send, sums_got, part_send, part_got, count_send, count_got, count_f, count_b,
    eye_perm,
    load_sem, h_send, h_got, x_send, x_got, s_send, s_got, rec_ssem, rec_rsem, sum_ssem, sum_rsem,
    part_ssem, part_rsem, cnt_ssem, cnt_rsem,
):
    tiles, mics, width = phase.shape
    scale = float(mics * mics - mics)
    row, col = lax.axis_index("row"), lax.axis_index("col")
    x, core = lax.div(row, 2), lax.rem(row, 2)
    y, z = lax.div(col, 4), lax.rem(col, 4)
    me = col * 4 + x
    other = row + 1 - 2 * core

    barrier = pltpu.get_barrier_semaphore()

    def greet(px, pc, pcore):
        pl.semaphore_signal(
            barrier, inc=1, device_id=(px * 2 + pcore, pc), device_id_type=MESH
        )

    for offset in OFFSETS[:22]:
        px, pc = lax.rem(x + offset[0], 4), lax.rem(y + offset[1], 4) * 4 + lax.rem(z + offset[2], 4)
        greet(px, pc, core)

    loads = [
        pltpu.make_async_copy(phase_hbm.at[0], phase.at[0], load_sem.at[0]),
        pltpu.make_async_copy(phase_hbm.at[1], phase.at[1], load_sem.at[1]),
        pltpu.make_async_copy(dirty_hbm, dirty, load_sem.at[2]),
        pltpu.make_async_copy(pairs_hbm, pairs, load_sem.at[3]),
        pltpu.make_async_copy(live_hbm, live, load_sem.at[4]),
    ]
    for load in loads:
        load.start()

    for offset in OFFSETS[22:]:
        px, pc = lax.rem(x + offset[0], 4), lax.rem(y + offset[1], 4) * 4 + lax.rem(z + offset[2], 4)
        greet(px, pc, core)
    for da in range(4):
        greet(lax.rem(x + da, 4), col, 1 - core)

    lane = lax.broadcasted_iota(jnp.int32, (8, 128), 1)
    sub = lax.broadcasted_iota(jnp.int32, (8, 128), 0)
    chip_lane = col * 4 + x

    def sums_record(estimate):
        record = jnp.zeros((8, 128), F32)
        for t in range(tiles):
            total = jnp.sum(estimate[t : t + 1, :], axis=1, keepdims=True)
            record = jnp.where((sub == 4 + core) & (lane == t * 64 + chip_lane), total, record)
        return record

    def form(estimate):
        mats = []
        row_id = lax.broadcasted_iota(jnp.int32, (mics, mics), 0)
        col_id = lax.broadcasted_iota(jnp.int32, (mics, mics), 1)
        for t in range(tiles):
            value = estimate[t : t + 1, :]
            total = jnp.sum(value, axis=1, keepdims=True)
            left = jnp.concatenate(
                [(esum[t] * value).astype(BF), (ediff[t] * -value).astype(BF)], axis=1
            )
            mat = dot(left, points[t])
            mats.append(jnp.where(row_id == col_id, mat - total, mat))
        return mats

    upper = lax.broadcasted_iota(jnp.int32, (32, 8, 128), 1) < 4

    def cut_by_chip(mats):
        for half in range(2):
            parts = [m[:, half * 128 : half * 128 + 128].reshape(32, 8, 128) for m in mats]
            send_h[pl.ds(half * 32, 32)] = jnp.concatenate(parts, axis=1).astype(BF)

    def cut_by_core(mats):
        for half in range(2):
            first, second = [m[:, half * 128 : half * 128 + 128].reshape(32, 8, 128) for m in mats]
            second = pltpu.roll(second, 4, 1)
            send_f[pl.ds(half * 32, 32), 0] = jnp.where(upper, first, second).astype(BF)
            send_f[pl.ds(half * 32, 32), 1] = jnp.where(upper, second, first).astype(BF)

    def send_each(src, dst, ssem, rsem, lead=False, midway=None):
        targets = []
        for da, db, dc in OFFSETS + [(0, 0, 0)]:
            px = lax.rem(x + da, 4)
            pc = lax.rem(y + db, 4) * 4 + lax.rem(z + dc, 4)
            for apart in range(2):
                if (da, db, dc) != (0, 0, 0) or apart:
                    targets.append((px * 2 + (1 - core if apart else core), pc))
        for place, ahead in enumerate(LEAD if lead else ()):
            first_row, first_col = targets[place]
            mine = (row == ahead) & (col == 0)
            moved = [(jnp.where(mine, first_row, ahead), jnp.where(mine, first_col, 0))]
            for prow, pcol in targets[place + 1 :]:
                hit = (prow == ahead) & (pcol == 0)
                moved.append((jnp.where(hit, first_row, prow), jnp.where(hit, first_col, pcol)))
            targets = targets[:place] + moved
        for place, (prow, pcol) in enumerate(targets):
            if midway is not None and place == 64:
                midway()
            slot, pcore = pcol * 4 + lax.div(prow, 2), lax.rem(prow, 2)
            apart = lax.rem(core + pcore, 2)
            pltpu.make_async_remote_copy(
                src_ref=src(slot, pcore, apart), dst_ref=dst(apart), send_sem=ssem, recv_sem=rsem,
                device_id=(prow, pcol), device_id_type=MESH,
            ).start()

    def send_all(src, dst, ssem, rsem):
        for da, db, dc in OFFSETS:
            px = lax.rem(x + da, 4)
            pc = lax.rem(y + db, 4) * 4 + lax.rem(z + dc, 4)
            pltpu.make_async_remote_copy(
                src_ref=src.at[pc * 4 + px], dst_ref=dst.at[me], send_sem=ssem, recv_sem=rsem,
                device_id=(px * 2 + core, pc), device_id_type=MESH,
            ).start()

    def send_row(src, dst, ssem, rsem):
        for k in (4, 5, 3, 2, 6, 7, 1):
            pltpu.make_async_remote_copy(
                src_ref=src, dst_ref=dst.at[row], send_sem=ssem, recv_sem=rsem,
                device_id=(lax.rem(row + k, 8), col), device_id_type=MESH,
            ).start()

    def send_col(src, dst, ssem, rsem):
        for da, db, dc in OFFSETS:
            if da == 0:
                pltpu.make_async_remote_copy(
                    src_ref=src, dst_ref=dst, send_sem=ssem, recv_sem=rsem,
                    device_id=(row, lax.rem(y + db, 4) * 4 + lax.rem(z + dc, 4)), device_id_type=MESH,
                ).start()

    def wait(ref, sem):
        pltpu.make_async_copy(ref, ref, sem).wait()

    loads[2].wait()
    powers, diags, firsts = [], [], []
    for t in range(tiles):
        loads[t].wait()
        angle = phase[t]
        square = angle * angle
        half_sine = polynomial(square, HALF_SIN) * angle
        twice = half_sine + half_sine
        cosine = (1.0 - twice * half_sine).astype(BF)
        sine = (twice * polynomial(square, HALF_COS)).astype(BF)
        cos_b[t] = cosine
        sin_b[t] = sine
        cosine, sine = cosine.astype(F32), sine.astype(F32)
        esum[t] = cosine + sine
        ediff[t] = cosine - sine
        power = jnp.sum(cosine * cosine + sine * sine, axis=0, keepdims=True)
        diag = (power * power - float(mics)) / scale
        powers.append(power)
        diags.append(diag)
        firsts.append(jnp.maximum(dirty[t : t + 1, :] / diag, 0.0))
        points[t] = jnp.concatenate([cosine.T, sine.T], axis=0).astype(BF)
    power = jnp.concatenate(powers, axis=0)
    diag = jnp.concatenate(diags, axis=0)
    estimate = jnp.concatenate(firsts, axis=0)

    loads[3].wait()
    loads[4].wait()
    slots = pairs.shape[1]
    first, second = pairs[0:1, :], pairs[1:2, :]
    first_lane = (first & 1) * 64 + ((first >> 1) & 15) * 4 + (first >> 6)
    second_row = (second >> 5) * 2 + (second & 1)
    listed = lax.broadcasted_iota(jnp.int32, (128, slots), 1) < live[0]
    first_hot = (lax.broadcasted_iota(jnp.int32, (128, slots), 0) == first_lane) & listed
    second_hot = lax.broadcasted_iota(jnp.int32, (16, slots), 0) == second_row
    part_send[...] = dot_nt(
        second_hot.astype(F32).astype(BF), first_hot.astype(F32).astype(BF)
    ).astype(BF)
    part_got[row] = part_send[...]
    record = sums_record(estimate)
    rec_send[0] = record
    rec_got[0, row] = record
    cut_by_chip(form(estimate))

    raw = lax.broadcasted_iota(jnp.int32, (256, 256), 1)
    raw_row = (raw >> 1) & 7
    placed = (((raw_row + core) & 1) << 7) + ((raw & 1) << 6) + ((raw >> 4) << 2) + (raw_row >> 1)
    eye_perm[...] = (lax.broadcasted_iota(jnp.int32, (256, 256), 0) == placed).astype(F32).astype(BF)

    pl.semaphore_wait(barrier, len(OFFSETS) + 4)

    for it in range(ITERS):
        if it == 0:
            send_row(part_send, part_got, part_ssem, part_rsem)
            send_all(send_h, own_h, h_send.at[0], h_got.at[0])
            own_h[me] = send_h[me]
            wait(part_got.at[pl.ds(0, 7)], part_rsem)
            by_core = [
                sum(part_got[2 * k + c].astype(F32) for k in range(4)).astype(BF) for c in range(2)
            ]
            count_send[:, 0:128] = jnp.where(core == 0, by_core[0], by_core[1])
            count_send[:, 128:256] = jnp.where(core == 0, by_core[1], by_core[0])
            here = pl.ds(pl.multiple_of(col * 16, 16), 16)
            count_got[here, :] = count_send[...]
            send_col(count_send, count_got.at[here], cnt_ssem, cnt_rsem)
            send_row(rec_send.at[0], rec_got.at[0], rec_ssem.at[0], rec_rsem.at[0])
            wait(own_h.at[pl.ds(0, 63)], h_got.at[0])
            exchange = pltpu.make_async_remote_copy(
                src_ref=own_h, dst_ref=other_h, send_sem=x_send, recv_sem=x_got,
                device_id=(other, col), device_id_type=MESH,
            )
            exchange.start()
        else:
            def send_sums():
                record = sums_record(estimate)
                rec_send[it] = record
                rec_got[it, row] = record
                send_row(rec_send.at[it], rec_got.at[it], rec_ssem.at[it], rec_rsem.at[it])

            send_each(
                lambda slot, pcore, apart: send_f.at[slot, pcore],
                lambda apart: in_f.at[apart * 64 + me],
                h_send.at[it], h_got.at[it], midway=send_sums,
            )
            in_f[me] = send_f[me, core]

        wait(rec_got.at[it, pl.ds(0, 7)], rec_rsem.at[it])
        record = jnp.sum(rec_got[it], axis=0)
        sums_send[it] = record
        sums_got[it, col] = record
        send_col(sums_send.at[it], sums_got.at[it, col], sum_ssem.at[it], sum_rsem.at[it])

        if it == 0:
            for base, source in ((0, own_h), (128, other_h)):
                if base:
                    exchange.wait_recv()
                turned = jnp.swapaxes(source[...], 0, 1)
                for k in range(16):
                    stack[base + (k // 8) * 64 : base + (k // 8) * 64 + 64,
                          (k % 8) * 128 : (k % 8) * 128 + 128] = turned[k]
            wait(count_got.at[pl.ds(0, 240)], cnt_rsem)
            ordered = dot(eye_perm[...], count_got[...])
            here_id = lax.broadcasted_iota(jnp.int32, (128, 256), 0)
            all_id = lax.broadcasted_iota(jnp.int32, (128, 256), 1)
            counts = ordered[0:128, :] + ordered[:, 0:128].T + (here_id == all_id).astype(F32)
            count_f[...] = counts
            count_b[0:128, :] = counts.astype(BF)
            total = dot(count_b[0:128, :], stack[...])
            cut = [
                total[(k // 8) * 64 : (k // 8) * 64 + 64, (k % 8) * 128 : (k % 8) * 128 + 128]
                for k in range(16)
            ]
            send_s[...] = jnp.swapaxes(jnp.stack(cut, axis=0), 0, 1).astype(BF)
            send_all(send_s, got_s, s_send.at[0], s_got.at[0])
            got_s[me] = send_s[me]
            counts = ordered[128:256, :] + ordered[:, 128:256].T + (here_id + 128 == all_id).astype(F32)
            count_b[128:256, :] = counts.astype(BF)
        else:
            wait(in_f.at[pl.ds(0, 127)], h_got.at[it])
            turned = jnp.swapaxes(in_f[...], 0, 1)
            for k in range(4):
                first = jnp.where(core == 0, turned[k], turned[4 + k])
                second = jnp.where(core == 0, turned[4 + k], turned[k])
                for apart in range(2):
                    stack[apart * 128 : apart * 128 + 64, k * 128 : k * 128 + 128] = first[
                        apart * 64 : apart * 64 + 64
                    ]
                    stack[apart * 128 + 64 : apart * 128 + 128, k * 128 : k * 128 + 128] = second[
                        apart * 64 : apart * 64 + 64
                    ]
            total = dot(count_b[...], stack[:, 0:512])
            for apart in range(2):
                part = total[apart * 128 : apart * 128 + 128]
                top = jnp.where(core == 0, part[0:64], part[64:128])
                low = jnp.where(core == 0, part[64:128], part[0:64])
                cut = [v[:, k * 128 : k * 128 + 128] for v in (top, low) for k in range(4)]
                out_f[apart * 64 : apart * 64 + 64] = jnp.swapaxes(jnp.stack(cut, axis=0), 0, 1).astype(BF)
            send_each(
                lambda slot, pcore, apart: out_f.at[apart * 64 + slot],
                lambda apart: got_f.at[me * 2 + core],
                s_send.at[it], s_got.at[it], lead=True,
            )
            got_f[me * 2 + core] = out_f[me]
        wait(sums_got.at[it, pl.ds(0, 15)], sum_rsem.at[it])
        sums = jnp.sum(sums_got[it], axis=0)
        own_sums = jnp.where(core == 0, sums[4:5, :], sums[5:6, :])
        other_sums = jnp.where(core == 0, sums[5:6, :], sums[4:5, :])
        partner = jnp.concatenate([own_sums, other_sums], axis=1)
        spread = [
            jnp.sum(count_f[pl.ds(t * 64 + chip_lane, 1), :] * partner, axis=1, keepdims=True)
            for t in range(tiles)
        ]

        if it == 0:
            wait(got_s.at[pl.ds(0, 63)], s_got.at[it])
        else:
            wait(got_f.at[pl.ds(0, 127)], s_got.at[it])
        news = []
        for t in range(tiles):
            halves = []
            for half in range(2):
                if it == 0:
                    block = got_s[half * 32 : half * 32 + 32].astype(F32)[:, t * 8 : t * 8 + 8, :]
                else:
                    pair = got_f[half * 64 : half * 64 + 64].astype(F32).reshape(32, 2, 8, 128)
                    block = jnp.where(upper, pair[:, t], pair[:, 1 - t])
                    if t:
                        block = pltpu.roll(block, 4, 1)
                halves.append(block.reshape(256, 128))
            mat = jnp.concatenate(halves, axis=1).astype(BF)
            form_sum = jnp.sum(
                esum[t] * dot(mat, cos_b[t]) - ediff[t] * dot(mat, sin_b[t]), axis=0, keepdims=True
            )
            value = (form_sum + spread[t] * (power[t : t + 1] - float(mics))) / scale
            old = estimate[t : t + 1]
            news.append(jnp.maximum(old + (dirty[t : t + 1, :] - value) / diag[t : t + 1], 0.0))
        estimate = jnp.concatenate(news, axis=0)
        if it + 1 < ITERS:
            cut_by_core(form(estimate))

    out_ref[...] = estimate
    wait(send_h.at[pl.ds(0, 63)], h_send.at[0])
    wait(other_h, x_send)
    wait(send_s.at[pl.ds(0, 63)], s_send.at[0])
    wait(in_f.at[pl.ds(0, 127)], h_send.at[1])
    wait(out_f.at[pl.ds(0, 127)], s_send.at[1])
    for it in range(ITERS):
        wait(rec_got.at[it, pl.ds(0, 7)], rec_ssem.at[it])
        wait(sums_got.at[it, pl.ds(0, 15)], sum_ssem.at[it])
    wait(count_got.at[pl.ds(0, 240)], cnt_ssem)
    wait(part_got.at[pl.ds(0, 7)], part_ssem)


def on_device(phase, dirty_map, pairs, live):
    tiles, mics, width = phase.shape
    vmem, dma = pltpu.VMEM, pltpu.SemaphoreType.DMA
    blocks, fine = vmem((64, 16, 128), BF), vmem((128, 8, 128), BF)
    return pl.pallas_call(
        kernel,
        out_shape=jax.ShapeDtypeStruct(dirty_map.shape, F32),
        in_specs=[pl.BlockSpec(memory_space=pl.ANY)] * 4,
        out_specs=pl.BlockSpec(memory_space=pltpu.VMEM),
        scratch_shapes=[
            vmem((tiles, mics, width), F32),
            vmem((tiles, width), F32),
            vmem((2, pairs.shape[0]), jnp.int32),
            pltpu.SMEM((1,), jnp.int32),
            vmem((tiles, mics, width), BF),
            vmem((tiles, mics, width), BF),
            vmem((tiles, 2 * width, mics), BF),
            vmem((tiles, mics, width), F32),
            vmem((tiles, mics, width), F32),
            blocks, blocks, blocks, blocks, blocks,
            vmem((64, 2, 8, 128), BF), fine, fine, fine,
            vmem((256, 1024), BF),
            vmem((ITERS, 8, 128), F32),
            vmem((ITERS, 8, 8, 128), F32),
            vmem((ITERS, 8, 128), F32),
            vmem((ITERS, 16, 8, 128), F32),
            vmem((16, 128), BF),
            vmem((8, 16, 128), BF),
            vmem((16, 256), BF),
            vmem((256, 256), BF),
            vmem((128, 256), F32),
            vmem((256, 256), BF),
            vmem((256, 256), BF),
            dma((5,)),
            dma((ITERS,)), dma((ITERS,)), dma, dma, dma((ITERS,)), dma((ITERS,)),
            dma((ITERS,)), dma((ITERS,)), dma((ITERS,)), dma((ITERS,)),
            dma, dma, dma, dma,
        ],
        compiler_params=pltpu.CompilerParams(
            collective_id=0, has_side_effects=True, vmem_limit_bytes=48 << 20
        ),
    )(*[pltpu.with_memory_space_constraint(v, pltpu.HBM) for v in (phase, dirty_map, pairs.T)], live)


def solution(mesh):
    in_specs = (
        P(("row", "col"), None, None),
        P(("row", "col"), None),
        P(("row", "col"), None),
        P(("row", "col")),
    )
    out_specs = P(("row", "col"), None)
    return jax.shard_map(
        on_device, mesh=mesh, in_specs=in_specs, out_specs=out_specs, check_vma=False
    )
```
